32 devices in a mesh: dp: 16 (over z, y, x), tensor: 2 (over core).
Axes of the slice: x: 2, y: 2, z: 4, core: 2. Of those that a mesh axis runs over, the one named last changes fastest.
Arguments:
- tokens: bfloat16 [2048, 2048], P('dp'), may hold values from -6 to 6
- cotangent: bfloat16 [2048, 2048], P('dp'), may hold values from -6 to 6
- expert_ids: int32 [2048, 4], P('dp'), may hold values from 0 to 15, all different within a row; in each aligned block of 128 rows (0 to 127, 128 to 255, ...) at most 40 rows name the same one
- route_weight: float32 [2048, 4], P('dp'), may hold values from 0.05 to 1
- forget_mask: int32 [2048], P('dp'), may hold values from 0 to 1, as said below
- lengths: int32 [2], replicated, may hold values from 256 to 1024, as said below
- gate_weight: bfloat16 [16, 1024, 2048], P('dp', 'tensor'), may hold values from -0.125 to 0.125
- up_weight: bfloat16 [16, 1024, 2048], P('dp', 'tensor'), may hold values from -0.125 to 0.125
- down_weight: bfloat16 [16, 1024, 2048], P('dp', 'tensor'), may hold values from -0.1875 to 0.1875
Outputs:
- mixed_out: bfloat16 [2048, 2048], P('dp', 'tensor')
- grad_gate: bfloat16 [16, 1024, 2048], P('dp', 'tensor')
- grad_up: bfloat16 [16, 1024, 2048], P('dp', 'tensor')
- grad_down: bfloat16 [16, 1024, 2048], P('dp', 'tensor')
The draws below stay inside these ranges and needn't reach their ends.
Inputs may be any that keep to these rules, and one draw needn't show every extreme that they name: `expert_ids`: among the rows of one index of dp (aligned blocks of 128 tokens), no expert is named more than 40 times. `forget_mask`: the first token slot of every sequence is 0 and the second is 1. `lengths`: at least one sequence uses all 1024 slots.
All inputs are finite; a program needn't handle non-finite values.
Results may differ from the reference program's by a relative error of at most 0.019.
Values may be sent and summed in bfloat16 or wider, within the bound.
No kernel may reach another device: no remote copies, remote signals or barrier semaphores. Data moves between devices by JAX's collectives and lax.ppermute only.
A program may use at most 128 MiB of HBM per device.

```python
import math
import jax
import jax.numpy as jnp
import numpy as np
from jax import lax

D = 2048
FFE = 1024
TOPK = 4
SEQS = 2
TOK_DEV = 128
EXPERTS = 16
SLICE = 512
CAP = 40
TOKENS = 2048
SEQ_LEN = 1024
N_DP = 16
N_TENSOR = 2


def draw_forget_mask(key, part):
    place = jnp.arange(TOKENS, dtype=jnp.int32)
    level = 150 + 450 * place // TOKENS
    rolled = jax.random.randint(key, (TOKENS,), 0, 1000)
    masked = (rolled < level).astype(jnp.int32)
    seq_pos = place % SEQ_LEN
    masked = jnp.where(seq_pos == 0, 0, jnp.where(seq_pos == 1, 1, masked))
    return masked.astype(jnp.int32)


def draw_lengths(key, part):
    first_key, second_key = jax.random.split(key)
    values = jax.random.randint(first_key, (SEQS,), SEQ_LEN // 4, SEQ_LEN + 1)
    chosen = jax.random.randint(second_key, (), 0, SEQS)
    return jnp.where(jnp.arange(SEQS) == chosen, SEQ_LEN, values).astype(jnp.int32)


def shard_levels(stream_key, dims, cuts, low, high):
    def one(position, parts):
        steps = jax.random.uniform(jax.random.fold_in(jax.random.fold_in(stream_key, 6), position), (parts,), jnp.float32, low / len(cuts), high / len(cuts))
        return jnp.repeat(jnp.exp(steps), dims[position] // parts).reshape((-1,) + (1,) * (len(dims) - position - 1))

    gain = one(*cuts[0])
    for cut in cuts[1:]:
        gain = gain * one(*cut)
    return gain


def routed_block(own_key, own, number, rows, number_of, top, reach, lean):
    order = jax.random.permutation(own_key, number_of)
    packed, usual = load_shares(number_of, rows * top, reach, lean, True), load_shares(number_of, rows * top, reach, lean, False)
    places = jnp.arange(number_of)

    def named(tallies, offset_by):
        used = int((tallies > 0).sum())
        fixed = max(1, used // 4)
        passed = fixed + (places - fixed + offset_by * (used - fixed)) % max(1, number_of - fixed)
        return jnp.zeros((number_of,), jnp.int32).at[order[jnp.where(places < fixed, places, passed)]].set(jnp.asarray(tallies, jnp.int32))

    tallies = jnp.where(number % 4 == 0, named(packed, number // 4), named(usual, number - number // 4 - 1))
    mixed = jax.random.permutation(jax.random.fold_in(own, 3), number_of)
    source_of, sink = mixed[0:number_of // 2 * 2:2], mixed[1:number_of // 2 * 2:2]
    margin = jnp.minimum(tallies[source_of] - 1, reach - tallies[sink]) // 2
    margin = jnp.where((source_of == order[0]) | (sink == order[0]) | (tallies[sink] == 0), 0, jnp.maximum(margin, 0))
    passed = jax.random.randint(jax.random.fold_in(own, 4), (number_of // 2,), 0, 1 << 20) % (margin + 1)
    tallies = tallies.at[source_of].add(-passed).at[sink].add(passed)
    items = jnp.searchsorted(jnp.cumsum(tallies), jnp.arange(rows * top), side="right").astype(jnp.int32)
    table = items.reshape(top, rows).T
    table = table[jax.random.permutation(jax.random.fold_in(own, 1), rows)]
    offset_by = jax.random.randint(jax.random.fold_in(own, 2), (rows, 1), 0, top)
    return jnp.take_along_axis(table, (jnp.arange(top)[None, :] + offset_by) % top, axis=1)


def load_shares(count, total, bound, slope, full):
    loads = [(1 << 20) // math.isqrt(grade ** slope) + 1 for grade in range(1, count + 1)]
    largest = bound if full else min(bound, max(-(-total // count), total * loads[0] // sum(loads)))
    least = 1 if total - largest >= count - 1 else 0
    given, rest = [largest] + [least] * (count - 1), total - largest - least * (count - 1)
    while rest > 0:
        candidates = [i for i in range(1, count) if given[i] < largest] or [i for i in range(1, count) if given[i] < bound]
        whole, left = sum([loads[i] for i in candidates]), rest
        for i in candidates:
            extra = min(bound - given[i], max(1, left * loads[i] // whole), rest)
            given[i] = given[i] + extra
            rest = rest - extra
    return np.array(given)


def centred(stream_key, shape, deviation, bound, cuts=(), kind=jnp.bfloat16):
    values = deviation * jax.random.normal(stream_key, shape, jnp.float32)
    if cuts:
        values = values * shard_levels(stream_key, shape, cuts, -0.22, 0.18)
    return jnp.clip(values, -bound, bound).astype(kind)


def setup_inputs(seed: int = 0) -> dict:
    splits = jax.random.split(jax.random.key(seed), 10)
    tokens = centred(splits[0], (TOKENS, D), 1.0, 6.0, ((0, 16),))
    cotangent = centred(splits[1], (TOKENS, D), 1.0, 6.0, ((0, 16),))
    expert_ids_keys = jax.random.split(jax.random.fold_in(splits[2], 1), TOKENS // TOK_DEV)
    expert_ids_turns = jax.random.permutation(jax.random.fold_in(splits[2], 3), TOKENS // TOK_DEV)
    expert_ids = jax.vmap(lambda own, number: routed_block(jax.random.fold_in(splits[2], 2), own, number, TOK_DEV, EXPERTS, TOPK, CAP, 2))(expert_ids_keys, expert_ids_turns).reshape((TOKENS, TOPK))
    route_weight = jnp.clip(jnp.exp(math.log(1.0) - 2.9957323 * jax.random.uniform(splits[3], (TOKENS, TOPK), jnp.float32) ** shard_levels(splits[3], (TOKENS, TOPK), ((0, 16),), -0.2, 0.2)), 0.05, 1.0)
    forget_mask = draw_forget_mask(jax.random.fold_in(splits[9], 71), 0)
    lengths = draw_lengths(jax.random.fold_in(splits[9], 71), 0)
    gate_weight = centred(splits[6], (EXPERTS, FFE, D), D ** -0.5, 0.125, ((0, 16), (1, 2)))
    up_weight = centred(splits[7], (EXPERTS, FFE, D), D ** -0.5, 0.125, ((0, 16), (1, 2)))
    down_weight = centred(splits[8], (EXPERTS, FFE, D), FFE ** -0.5, 0.1875, ((0, 16), (1, 2)))
    return dict(tokens=tokens, cotangent=cotangent, expert_ids=expert_ids, route_weight=route_weight, forget_mask=forget_mask, lengths=lengths, gate_weight=gate_weight, up_weight=up_weight, down_weight=down_weight)


def reference(tokens, cotangent, expert_ids, route_weight, forget_mask, lengths, gate_weight, up_weight, down_weight):
    total_rows = tokens.shape[0]
    token_index = jnp.arange(total_rows, dtype=jnp.int32)
    seq_id = token_index // SEQ_LEN
    seq_pos = token_index - seq_id * SEQ_LEN
    is_valid = (seq_pos < lengths[seq_id]).astype(jnp.int32)
    forget = is_valid * forget_mask
    retain = is_valid - forget
    n_forget = jnp.sum(forget).astype(jnp.float32)
    n_retain = jnp.sum(retain).astype(jnp.float32)
    coefficient = float(TOPK * TOK_DEV) * (retain.astype(jnp.float32) / n_retain - forget.astype(jnp.float32) / n_forget)
    shares = route_weight / jnp.sum(route_weight, axis=1, keepdims=True)
    share_flat = shares.reshape(-1)
    flat_ids = expert_ids.reshape(-1)
    sorted_ids = jnp.argsort(flat_ids, stable=True).astype(jnp.int32)
    counts = jnp.sum((flat_ids[:, None] == jnp.arange(EXPERTS, dtype=jnp.int32)[None, :]).astype(jnp.int32), axis=0)
    starts = (jnp.cumsum(counts) - counts).astype(jnp.int32)
    row_count = N_DP * CAP
    padded_ids = jnp.concatenate([sorted_ids, jnp.zeros((row_count,), jnp.int32)])

    def expert_step(mixed_sum, expert):
        slot_ids = lax.dynamic_slice_in_dim(padded_ids, starts[expert], row_count)
        is_live = jnp.arange(row_count, dtype=jnp.int32) < counts[expert]
        tok_ids = slot_ids // TOPK
        rows_in = jnp.where(is_live[:, None], tokens[tok_ids], jnp.zeros((), tokens.dtype))
        weight = jnp.where(is_live, share_flat[slot_ids], jnp.zeros((), share_flat.dtype))
        routed = ((coefficient[tok_ids] * weight)[:, None] * cotangent[tok_ids].astype(jnp.float32)).astype(jnp.bfloat16)
        gate_pre = jnp.dot(rows_in, gate_weight[expert].T, preferred_element_type=jnp.float32)
        up_pre = jnp.dot(rows_in, up_weight[expert].T, preferred_element_type=jnp.float32)
        sigmoid_gate = jax.nn.sigmoid(gate_pre)
        hidden = (gate_pre * sigmoid_gate * up_pre).astype(jnp.bfloat16)
        pieces = jnp.einsum("rns,nsd->rnd", hidden.reshape(row_count, N_TENSOR, SLICE).astype(jnp.float32),
                            down_weight[expert].reshape(N_TENSOR, SLICE, -1).astype(jnp.float32))
        rounded = lax.optimization_barrier(pieces.astype(jnp.bfloat16))
        expert_out = jnp.sum(rounded.astype(jnp.float32), axis=1)
        mixed_sum = mixed_sum.at[tok_ids].add(weight[:, None] * expert_out)
        grad_down = jnp.dot(hidden.T, routed, preferred_element_type=jnp.float32)
        dhidden = jnp.dot(routed, down_weight[expert].T, preferred_element_type=jnp.float32)
        dgate = (dhidden * up_pre * sigmoid_gate * (1.0 + gate_pre * (1.0 - sigmoid_gate))).astype(jnp.bfloat16)
        dup = (dhidden * gate_pre * sigmoid_gate).astype(jnp.bfloat16)
        grad_gate = jnp.dot(dgate.T, rows_in, preferred_element_type=jnp.float32)
        grad_up = jnp.dot(dup.T, rows_in, preferred_element_type=jnp.float32)
        return mixed_sum, (grad_gate.astype(jnp.bfloat16), grad_up.astype(jnp.bfloat16), grad_down.astype(jnp.bfloat16))

    mixed_sum, grad_all = lax.scan(expert_step, jnp.zeros((total_rows, D), jnp.float32), jnp.arange(EXPERTS, dtype=jnp.int32))
    return (mixed_sum.astype(jnp.bfloat16), grad_all[0], grad_all[1], grad_all[2])
```

```python
import jax
import jax.numpy as jnp
from jax import lax
from jax.sharding import PartitionSpec as P

F32 = jnp.float32
BF16 = jnp.bfloat16
META = 128


def dot(a, b, dims):
    return lax.dot_general(a, b, (dims, ((), ())), preferred_element_type=F32)


def body(
    tokens,
    cotangent,
    expert_ids,
    route_weight,
    forget_mask,
    lengths,
    gate_weight,
    up_weight,
    down_weight,
):
    tok_rows, features = tokens.shape
    top_count = expert_ids.shape[1]
    owners = lax.axis_size("dp")
    parts = lax.axis_size("tensor")
    half = owners // 2
    width = features // parts
    capacity = 5 * tok_rows * top_count // (4 * owners)
    slots = half * capacity
    me = lax.axis_index("dp")
    core = lax.axis_index("tensor")
    mates = [(i, (i + half) % owners) for i in range(owners)]
    halves = [list(range(half)), list(range(half, owners))]

    def to_mate(value):
        return lax.ppermute(value, "dp", mates)

    def exchange(value):
        return lax.all_to_all(
            value, "dp", split_axis=0, concat_axis=0, axis_index_groups=halves, tiled=True
        )

    def whole_rows(mine):
        if parts != 2:
            return lax.all_gather(mine, "tensor", axis=1, tiled=True)
        other = lax.ppermute(mine, "tensor", [(0, 1), (1, 0)])
        return jnp.where(
            core == 0,
            jnp.concatenate([mine, other], axis=1),
            jnp.concatenate([other, mine], axis=1),
        )

    def sum_rows(partial):
        if parts != 2:
            return lax.psum_scatter(partial, "tensor", scatter_dimension=1, tiled=True)
        low, high = partial[:, :width], partial[:, width:]
        other = lax.ppermute(jnp.where(core == 0, high, low), "tensor", [(0, 1), (1, 0)])
        mine = jnp.where(core == 0, low, high)
        return (mine.astype(F32) + other.astype(F32)).astype(BF16)

    def my_features(value):
        return lax.dynamic_slice_in_dim(value, core * width, width, axis=1)

    seq_count = lengths.shape[0]
    seq_len = tok_rows * owners // seq_count
    token_index = me * tok_rows + jnp.arange(tok_rows, dtype=jnp.int32)
    seq_id = token_index // seq_len
    seq_pos = token_index - seq_id * seq_len
    in_seq = seq_id[:, None] == jnp.arange(seq_count, dtype=jnp.int32)[None, :]
    limits = jnp.sum(jnp.where(in_seq, lengths[None, :], 0), axis=1)
    is_valid = (seq_pos < limits).astype(jnp.int32)
    forget = is_valid * forget_mask
    retain = is_valid - forget
    shares = route_weight / jnp.sum(route_weight, axis=1, keepdims=True)
    about = jnp.concatenate(
        [
            expert_ids.astype(F32).T,
            shares.T,
            retain.astype(F32)[None, :],
            forget.astype(F32)[None, :],
        ],
        axis=0,
    )
    about_mate = to_mate(about)
    tok_mine = my_features(tokens)
    tok_mate = to_mate(tok_mine)

    first = (me // half) * half
    expert = (first + jnp.arange(half, dtype=jnp.int32)).astype(F32)
    place = jnp.arange(tok_rows, dtype=jnp.int32)
    earlier = (place[:, None] < place[None, :]).astype(BF16)

    def slot_tables(info):
        hit = info[None, :top_count, :] == expert[:, None, None]
        named = jnp.any(hit, axis=1)
        weight = jnp.sum(jnp.where(hit, info[None, top_count : 2 * top_count, :], 0.0), axis=1)
        rank = dot(named.astype(BF16), earlier, ((1,), (0,)))
        rank = jnp.where(named, rank, -1.0)
        at_slot = rank[:, None, :] == jnp.arange(capacity, dtype=jnp.int32).astype(F32)[None, :, None]
        pick = at_slot.astype(BF16).reshape(slots, tok_rows)
        spread = jnp.where(at_slot, weight[:, None, :], 0.0).astype(BF16).reshape(slots, tok_rows)
        return pick, spread

    def split3(value):
        high = lax.reduce_precision(value, 8, 7)
        rest = value - high
        middle = lax.reduce_precision(rest, 8, 7)
        return [high, middle, rest - middle]

    def columns(info):
        share = info[top_count : 2 * top_count]
        rows = jnp.concatenate(
            [info[:top_count]] + split3(share) + [info[2 * top_count : 2 * top_count + 2]], axis=0
        )
        rows = jnp.pad(rows, ((0, META - rows.shape[0]), (0, 0)))
        return rows.T.astype(BF16)

    pick_own, spread_own = slot_tables(about)
    send_own = dot(pick_own, tok_mine, ((1,), (0,))).astype(BF16)
    recv_own = exchange(send_own.reshape(half, capacity, width)).reshape(slots, width)
    pick_mate, spread_mate = slot_tables(about_mate)
    send_mate = dot(pick_mate, tok_mate, ((1,), (0,))).astype(BF16)
    recv_mate = exchange(send_mate.reshape(half, capacity, width)).reshape(slots, width)

    cot_mine = my_features(cotangent)
    cot_mate = to_mate(cot_mine)
    count_at = 4 * top_count + 2
    counts = jnp.sum(about[2 * top_count :] + about_mate[2 * top_count :], axis=1)
    count_row = jnp.zeros((META,), F32).at[count_at].set(counts[0]).at[count_at + 1].set(counts[1])

    def cot_rows(pick, cot, info):
        rows = dot(pick, cot, ((1,), (0,))).astype(BF16)
        facts = (dot(pick, columns(info), ((1,), (0,))) + count_row[None, :]).astype(BF16)
        return jnp.concatenate([rows, facts], axis=1).reshape(half, capacity, width + META)

    send_cot = jnp.concatenate(
        [cot_rows(pick_own, cot_mine, about), cot_rows(pick_mate, cot_mate, about_mate)], axis=1
    )
    recv_cot = exchange(send_cot)

    gate_w, up_w, down_w = gate_weight[0], up_weight[0], down_weight[0]

    def forward(rows):
        gate_pre = dot(rows, gate_w, ((1,), (1,)))
        up_pre = dot(rows, up_w, ((1,), (1,)))
        sigmoid_gate = jax.nn.sigmoid(gate_pre)
        hidden = (gate_pre * sigmoid_gate * up_pre).astype(BF16)
        partial = dot(hidden, down_w, ((1,), (0,))).astype(BF16)
        return gate_pre, up_pre, hidden, sum_rows(partial)

    rows_own = whole_rows(recv_own)
    gate_own, up_own, hidden_own, out_own = forward(rows_own)
    rows_mate = whole_rows(recv_mate)
    gate_mate, up_mate, hidden_mate, out_mate = forward(rows_mate)

    back_mate = exchange(out_mate.reshape(half, capacity, width)).reshape(slots, width)
    mix_mate = dot(spread_mate, back_mate, ((0,), (0,))).astype(BF16)
    mix_far = to_mate(mix_mate)
    back_own = exchange(out_own.reshape(half, capacity, width)).reshape(slots, width)
    mixed = dot(spread_own, back_own, ((0,), (0,))) + mix_far.astype(F32)

    facts = recv_cot[:, :, width:].astype(F32)
    totals = jnp.sum(facts[:, 0, count_at : count_at + 2], axis=0)
    mine = facts[:, :, :top_count] == me.astype(F32)
    share = sum(facts[:, :, (1 + i) * top_count : (2 + i) * top_count] for i in range(3))
    share = jnp.sum(jnp.where(mine, share, 0.0), axis=2)
    flag_at = 4 * top_count
    coefficient = float(top_count * tok_rows) * (
        facts[:, :, flag_at] / totals[0] - facts[:, :, flag_at + 1] / totals[1]
    )
    slot_weight = coefficient * share
    routed = (slot_weight[:, :, None] * recv_cot[:, :, :width].astype(F32)).astype(BF16)
    routed = jnp.concatenate(
        [
            routed[:, :capacity].reshape(slots, width),
            routed[:, capacity:].reshape(slots, width),
        ],
        axis=0,
    )
    routed = whole_rows(routed)

    def joined(a, b):
        return jnp.concatenate([a, b], axis=0)

    hidden = joined(hidden_own, hidden_mate)
    rows_in = joined(rows_own, rows_mate)
    gate_pre = joined(gate_own, gate_mate)
    up_pre = joined(up_own, up_mate)
    sigmoid_gate = jax.nn.sigmoid(gate_pre)
    grad_down = dot(hidden, routed, ((0,), (0,)))
    dhidden = dot(routed, down_w, ((1,), (1,)))
    dgate = (dhidden * up_pre * sigmoid_gate * (1.0 + gate_pre * (1.0 - sigmoid_gate))).astype(BF16)
    dup = (dhidden * gate_pre * sigmoid_gate).astype(BF16)
    grad_gate = dot(dgate, rows_in, ((0,), (0,)))
    grad_up = dot(dup, rows_in, ((0,), (0,)))
    return (
        mixed.astype(BF16),
        grad_gate.astype(BF16)[None],
        grad_up.astype(BF16)[None],
        grad_down.astype(BF16)[None],
    )


def solution(mesh):
    in_specs = (
        P("dp", None),
        P("dp", None),
        P("dp", None),
        P("dp", None),
        P("dp"),
        P(),
        P("dp", "tensor", None),
        P("dp", "tensor", None),
        P("dp", "tensor", None),
    )
    out_specs = (
        P("dp", "tensor"),
        P("dp", "tensor", None),
        P("dp", "tensor", None),
        P("dp", "tensor", None),
    )
    return jax.shard_map(body, mesh=mesh, in_specs=in_specs, out_specs=out_specs, check_vma=False)
```

```python
import functools

import jax
import jax.numpy as jnp
from jax import lax
from jax.experimental import pallas as pl
from jax.experimental.pallas import tpu as pltpu
from jax.sharding import PartitionSpec as P

F32 = jnp.float32
BF16 = jnp.bfloat16
LANES = 128
FACTS = 16
VMEM = pl.BlockSpec(memory_space=pltpu.VMEM)
SMEM = pl.BlockSpec(memory_space=pltpu.SMEM)
ANY = pl.BlockSpec(memory_space=pl.ANY)
HBM = pl.BlockSpec(memory_space=pltpu.HBM)


def cost(micros):
    return pl.CostEstimate(
        flops=int(micros * 1e9), bytes_accessed=int(micros * 3e6), transcendentals=0
    )


def in_hbm(value):
    return pltpu.with_memory_space_constraint(value, pltpu.HBM)


def dot(a, b, dims):
    return lax.dot_general(a, b, (dims, ((), ())), preferred_element_type=F32)


def facts_kernel(top, seq_len, place_ref, lengths_ref, ids_ref, weight_ref, forget_ref, out_ref):
    toks = ids_ref.shape[1]
    weight = weight_ref[...]
    out_ref[:top, :] = ids_ref[...].astype(F32)
    out_ref[top : 2 * top, :] = weight / jnp.sum(weight, axis=0, keepdims=True)
    token = place_ref[0] + lax.broadcasted_iota(jnp.int32, (1, toks), 1)
    valid = jnp.zeros((1, toks), jnp.int32)
    for s in range(lengths_ref.shape[0]):
        begin = s * seq_len
        inside = (token >= begin) & (token < begin + lengths_ref[s])
        valid = jnp.where(inside, 1, valid)
    forget = valid * forget_ref[...]
    out_ref[2 * top : 2 * top + 1, :] = (valid - forget).astype(F32)
    out_ref[2 * top + 1 : 2 * top + 2, :] = forget.astype(F32)
    rest = 2 * top + 2
    out_ref[rest:, :] = jnp.zeros((out_ref.shape[0] - rest, toks), F32)


def slot_tables(top, half, capacity, first, info, pick_ref, weighted_ref=None, factor=None):
    toks = info.shape[1]
    expert = (first + lax.broadcasted_iota(jnp.int32, (half, toks), 0)).astype(F32)
    named = jnp.zeros((half, toks), F32)
    weight = jnp.zeros((half, toks), F32)
    for k in range(top):
        hit = info[k : k + 1, :] == expert
        named = jnp.where(hit, 1.0, named)
        weight = jnp.where(hit, info[top + k : top + k + 1, :], weight)
    row = lax.broadcasted_iota(jnp.int32, (toks, toks), 0)
    column = lax.broadcasted_iota(jnp.int32, (toks, toks), 1)
    earlier = jnp.where(row < column, 1.0, 0.0).astype(BF16)
    rank = dot(named.astype(BF16), earlier, ((1,), (0,)))
    rank = jnp.where(named > 0.0, rank, -1.0)
    if factor is not None:
        weight = factor * weight
    slot = lax.broadcasted_iota(jnp.int32, (capacity, toks), 0).astype(F32)
    for e in range(half):
        at = rank[e : e + 1, :] == slot
        rows = slice(e * capacity, (e + 1) * capacity)
        pick_ref[rows, :] = jnp.where(at, 1.0, 0.0)
        if weighted_ref is not None:
            weighted_ref[rows, :] = jnp.where(at, weight[e : e + 1, :], 0.0)


def gather_kernel(top, half, capacity, counted, first_ref, info_ref, x_ref, out_ref, pick_ref):
    info = info_ref[...]
    width = x_ref.shape[1]
    slot_tables(top, half, capacity, first_ref[0], info, pick_ref)
    out_ref[:, :width] = dot(pick_ref[...].astype(BF16), x_ref[...], ((1,), (0,))).astype(BF16)
    if counted:
        count = jnp.sum(info[2 * top : 2 * top + 2, :], axis=1, keepdims=True)
        lane = lax.broadcasted_iota(jnp.int32, (out_ref.shape[0], LANES), 1)
        both = jnp.where(lane == 0, count[0:1, :], jnp.where(lane == 1, count[1:2, :], 0.0))
        out_ref[:, width:] = both.astype(BF16)


def scaled_kernel(
    top, half, capacity, scale, first_ref, total_ref, info_ref, info2_ref, x_ref, x2_ref, out_ref, pick_ref, weight_ref
):
    width = x_ref.shape[1]
    total = total_ref[...]
    retain_all, forget_all = total[:, 0:1], total[:, 1:2]
    for i, (own, x) in enumerate(((info_ref, x_ref), (info2_ref, x2_ref))):
        info = own[...]
        factor = scale * (
            info[2 * top : 2 * top + 1, :] / retain_all - info[2 * top + 1 : 2 * top + 2, :] / forget_all
        )
        slot_tables(top, half, capacity, first_ref[0], info, pick_ref, weight_ref, factor)
        rows = dot(pick_ref[...].astype(BF16), x[...], ((1,), (0,)))
        slot_weight = jnp.sum(weight_ref[...], axis=1, keepdims=True)
        out_ref[:, i * width : (i + 1) * width] = (slot_weight * rows).astype(BF16)


def mix_kernel(top, half, capacity, first_ref, info_ref, back_ref, *rest):
    far_refs, (out_ref, pick_ref, weight_ref) = rest[:-3], rest[-3:]
    slot_tables(top, half, capacity, first_ref[0], info_ref[...], pick_ref, weight_ref)
    weight = weight_ref[...]
    high = weight.astype(BF16)
    low = (weight - high.astype(F32)).astype(BF16)
    back = back_ref[...]
    total = dot(high, back, ((0,), (0,))) + dot(low, back, ((0,), (0,)))
    for far in far_refs:
        total = total + far[...].astype(F32)
    out_ref[...] = total.astype(BF16)


def halve_kernel(core_ref, x_ref, out_ref):
    width = out_ref.shape[1]
    out_ref[...] = x_ref[:, pl.ds(pl.multiple_of(core_ref[0] * width, LANES), width)]


def add_kernel(a_ref, b_ref, out_ref):
    out_ref[...] = (a_ref[...].astype(F32) + b_ref[...].astype(F32)).astype(BF16)


def spans_of(at_ref, pieces, width):
    return [pl.ds(pl.multiple_of(at_ref[i], LANES), width) for i in range(pieces)]


def copier(sems):
    started = []

    def copy(src, dst):
        started.append(pltpu.make_async_copy(src, dst, sems.at[len(started)]))
        started[-1].start()
        return started[-1]

    return copy


def block(ref, j, step):
    return ref.at[pl.ds(j * step, step)]


def forward_kernel(pieces, step, at_ref, *refs):
    n = pieces
    xs_in, weights_in, refs = refs[: 2 * n], refs[2 * n : 2 * n + 3], refs[2 * n + 3 :]
    outs, refs = refs[: 3 + 2 * n], refs[3 + 2 * n :]
    xs, (gate_w, up_w, down_w), refs = refs[: 2 * n], refs[2 * n : 2 * n + 3], refs[2 * n + 3 :]
    held, sems = refs[:-1], refs[-1]
    keep_gate, keep_up, hidden_ref = held[:3]
    copy = copier(sems)
    slots, width = held[3].shape
    spans = spans_of(at_ref, n, width)
    blocks = gate_w.shape[0] // step
    x_copies = [copy(src.at[:, pl.ds(0, width)], dst) for src, dst in zip(xs_in, xs)]
    gate_copies, up_copies, down_copies = [], [], []
    for j in range(blocks):
        gate_copies.append(copy(block(weights_in[0], j, step), block(gate_w, j, step)))
        up_copies.append(copy(block(weights_in[1], j, step), block(up_w, j, step)))
    down_copy = copy(weights_in[2], down_w)
    for started in x_copies:
        started.wait()
    for j in range(blocks):
        gate_copies[j].wait()
        up_copies[j].wait()
        units = slice(j * step, (j + 1) * step)
        for part in (1, 0):
            rows = slice(part * slots, (part + 1) * slots)
            mine = xs[part * n : (part + 1) * n]
            gate = sum(dot(x[...], gate_w[units, span], ((1,), (1,))) for x, span in zip(mine, spans))
            up = sum(dot(x[...], up_w[units, span], ((1,), (1,))) for x, span in zip(mine, spans))
            s = jax.nn.sigmoid(gate)
            silu = gate * s
            keep_gate[rows, units] = (up * s * (1.0 + gate * (1.0 - s))).astype(BF16)
            keep_up[rows, units] = silu.astype(BF16)
            hidden_ref[rows, units] = (silu * up).astype(BF16)
    out_copies = [copy(src, dst) for src, dst in zip(held[:3], outs[:3])]
    down_copy.wait()
    for k, part in enumerate((1, 0)):
        hidden = hidden_ref[part * slots : (part + 1) * slots, :]
        for i in reversed(range(n)):
            spot = 3 + k * n + i
            held[spot][...] = dot(hidden, down_w[:, spans[i]], ((1,), (0,))).astype(BF16)
            out_copies.append(copy(held[spot], outs[spot]))
    for started in out_copies:
        started.wait()


def backward_kernel(pieces, step, at_ref, *refs):
    n = pieces
    xs_in, (weight_in, gate_in, up_in), refs = refs[:n], refs[n : n + 3], refs[n + 3 :]
    outs, xs, refs = refs[:2], refs[2 : 2 + n], refs[2 + n :]
    down_w, keep_gate, keep_up, dgate_ref, dup_ref, sems = refs
    copy = copier(sems)
    slots, width = xs[0].shape[0], xs[0].shape[1] // 2
    spans = spans_of(at_ref, n, width)
    blocks = down_w.shape[0] // step
    copies = [copy(src, dst) for src, dst in zip(xs_in, xs)]
    w_copies = [copy(block(weight_in, j, step), block(down_w, j, step)) for j in range(blocks)]
    copies += [copy(gate_in, keep_gate), copy(up_in, keep_up)]
    for started in copies:
        started.wait()
    for j in range(blocks):
        w_copies[j].wait()
        units = slice(j * step, (j + 1) * step)
        for part in range(2):
            rows = slice(part * slots, (part + 1) * slots)
            lanes = slice(part * width, (part + 1) * width)
            dhidden = sum(dot(x[:, lanes], down_w[units, span], ((1,), (1,))) for x, span in zip(xs, spans))
            dgate_ref[rows, units] = (dhidden * keep_gate[rows, units].astype(F32)).astype(BF16)
            dup_ref[rows, units] = (dhidden * keep_up[rows, units].astype(F32)).astype(BF16)
    for started in [copy(dgate_ref, outs[0]), copy(dup_ref, outs[1])]:
        started.wait()


def grads_kernel(joined, pieces, count, width, step, at_ref, *refs):
    n = pieces
    number = n if joined else 2 * n
    lefts_in, xs_in, refs = refs[:count], refs[count : count + number], refs[count + number :]
    outs, refs = refs[:count], refs[count:]
    lefts, xs, (turned, buffer, sems, out_sems) = refs[:count], refs[count : count + number], refs[count + number :]
    copy = copier(sems)
    slots = xs[0].shape[0]
    left_copies = [copy(src, dst) for src, dst in zip(lefts_in, lefts)]
    lanes = xs[0].shape[1]
    x_copies = [copy(src.at[:, pl.ds(0, lanes)], dst) for src, dst in zip(xs_in, xs)]
    copies, number = [None, None], 0
    for m in range(count):
        left_copies[m].wait()
        turned[...] = lefts[m][...].T
        if m == 0:
            for started in x_copies:
                started.wait()
        for i in range(n):
            for begin in range(0, width, step):
                total = 0.0
                for part in range(2):
                    rows = slice(part * slots, (part + 1) * slots)
                    if joined:
                        right = xs[i][:, part * width + begin : part * width + begin + step]
                    else:
                        right = xs[part * n + i][:, begin : begin + step]
                    total = total + dot(turned[:, rows], right, ((1,), (0,)))
                spot = number % 2
                if copies[spot] is not None:
                    copies[spot].wait()
                buffer[spot] = total.astype(BF16)
                target = pl.ds(pl.multiple_of(at_ref[i] + begin, LANES), step)
                copies[spot] = pltpu.make_async_copy(buffer.at[spot], outs[m].at[:, target], out_sems.at[spot])
                copies[spot].start()
                number += 1
    for started in copies:
        if started is not None:
            started.wait()


def body(
    tokens,
    cotangent,
    expert_ids,
    route_weight,
    forget_mask,
    lengths,
    gate_weight,
    up_weight,
    down_weight,
):
    tok_rows, features = tokens.shape
    top = expert_ids.shape[1]
    owners = lax.axis_size("dp")
    parts = lax.axis_size("tensor")
    half = owners // 2
    width = features // parts
    capacity = 5 * tok_rows * top // (4 * owners)
    slots = half * capacity
    seq_len = tok_rows * owners // lengths.shape[0]
    me = lax.axis_index("dp")
    core = lax.axis_index("tensor")
    mates = [(i, (i + half) % owners) for i in range(owners)]
    halves = [list(range(half)), list(range(half, owners))]
    first = ((me // half) * half).astype(jnp.int32).reshape(1)
    place = (me * tok_rows).astype(jnp.int32).reshape(1)
    table = pltpu.VMEM((slots, tok_rows), F32)
    limit = pltpu.CompilerParams(vmem_limit_bytes=8 * 2**20)

    def to_mate(value):
        return lax.ppermute(value, "dp", mates)

    def exchange(value):
        value = value.reshape(half, value.shape[0] // half, value.shape[1])
        return lax.all_to_all(
            value, "dp", split_axis=0, concat_axis=0, axis_index_groups=halves, tiled=True
        )

    def swapped(value):
        return lax.ppermute(value, "tensor", [(0, 1), (1, 0)])

    def my_features(value):
        return pl.pallas_call(
            halve_kernel,
            out_shape=jax.ShapeDtypeStruct((tok_rows, width), BF16),
            in_specs=[SMEM, VMEM],
            out_specs=VMEM,
            compiler_params=limit,
            cost_estimate=cost(1),
        )(core.astype(jnp.int32).reshape(1), value)

    def after(value, *others):
        return lax.optimization_barrier((value, *others))[0]

    def mixed_rows(info, back, *far):
        return pl.pallas_call(
            functools.partial(mix_kernel, top, half, capacity),
            out_shape=jax.ShapeDtypeStruct((tok_rows, width), BF16),
            in_specs=[SMEM, VMEM, VMEM] + [VMEM] * len(far),
            out_specs=VMEM,
            scratch_shapes=[table, table],
            compiler_params=limit,
            cost_estimate=cost(1),
        )(first, info, back, *far)

    tok_mine = my_features(tokens)
    tok_mate = to_mate(tok_mine)
    expert_ids = after(expert_ids, tok_mine)
    about = pl.pallas_call(
        functools.partial(facts_kernel, top, seq_len),
        out_shape=jax.ShapeDtypeStruct((FACTS, tok_rows), F32),
        in_specs=[SMEM, SMEM, VMEM, VMEM, VMEM],
        out_specs=VMEM,
        compiler_params=limit,
        cost_estimate=cost(1),
    )(place, lengths, expert_ids.T, route_weight.T, forget_mask.reshape(1, tok_rows))
    about_mate = to_mate(about)

    def gathered(info, x, counted, micros):
        return pl.pallas_call(
            functools.partial(gather_kernel, top, half, capacity, counted),
            out_shape=jax.ShapeDtypeStruct((slots, width + (LANES if counted else 0)), BF16),
            in_specs=[SMEM, VMEM, VMEM],
            out_specs=VMEM,
            scratch_shapes=[table],
            compiler_params=limit,
            cost_estimate=cost(micros),
        )(first, info, x)

    recv_own = exchange(gathered(about, tok_mine, True, 1))
    count = jnp.sum(recv_own[:, :1, width:].astype(F32), axis=0)
    total = count + to_mate(count)
    recv_own = recv_own.reshape(slots, width + LANES)
    recv_mate = exchange(gathered(about_mate, tok_mate, False, 1)).reshape(slots, width)

    cot_mine = my_features(after(cotangent, about))
    cot_mate = to_mate(cot_mine)
    send_cot = pl.pallas_call(
        functools.partial(scaled_kernel, top, half, capacity, float(top * tok_rows)),
        out_shape=jax.ShapeDtypeStruct((slots, 2 * width), BF16),
        in_specs=[SMEM] + [VMEM] * 5,
        out_specs=VMEM,
        scratch_shapes=[table, table],
        compiler_params=limit,
        cost_estimate=cost(1),
    )(first, total, about, about_mate, cot_mine, cot_mate)
    recv_cot = exchange(after(send_cot, recv_mate)).reshape(slots, 2 * width)

    gate_w, up_w, down_w = gate_weight[0], up_weight[0], down_weight[0]

    units = gate_w.shape[0]
    pieces = 2 if parts == 2 else 1
    span = features // pieces
    step = min(units, 256)
    blocks = units // step
    if parts == 2:
        at = jnp.stack([core, 1 - core]).astype(jnp.int32) * width
    else:
        at = jnp.zeros((1,), jnp.int32)
    shape = jax.ShapeDtypeStruct
    weight_buffer = pltpu.VMEM((units, features), BF16)
    roomy = pltpu.CompilerParams(vmem_limit_bytes=20 * 2**20)

    def pair(value):
        if parts == 2:
            return [value, swapped(value)]
        return [lax.all_gather(value[:, :width], "tensor", axis=1, tiled=True)]

    def double_pair(value):
        if parts == 2:
            return [value, swapped(value)]
        return [jnp.concatenate([pair(value[:, :width])[0], pair(value[:, width:])[0]], axis=1)]

    def summed(outs):
        if parts != 2:
            return lax.psum_scatter(outs[0], "tensor", scatter_dimension=1, tiled=True)
        return pl.pallas_call(
            add_kernel,
            out_shape=shape((slots, width), BF16),
            in_specs=[VMEM] * 2,
            out_specs=VMEM,
            compiler_params=limit,
            cost_estimate=cost(1),
        )(outs[0], swapped(outs[1]))

    toks = [in_hbm(x) for x in pair(recv_own) + pair(after(recv_mate, cot_mate))]
    weights = [in_hbm(w) for w in (gate_w, up_w, down_w)]
    kept = [((2 * slots, units), BF16)] * 3 + [((slots, span), BF16)] * (2 * pieces)
    held = [pltpu.VMEM(*k) for k in kept]
    x_buffers = [pltpu.VMEM((slots, span), BF16) for x in toks]
    keep_gate, keep_up, hidden, *outs = pl.pallas_call(
        functools.partial(forward_kernel, pieces, step),
        out_shape=[pltpu.HBM(*k) for k in kept],
        in_specs=[SMEM] + [HBM] * (2 * pieces + 3),
        out_specs=[HBM] * len(kept),
        scratch_shapes=x_buffers
        + [weight_buffer] * 3
        + held
        + [pltpu.SemaphoreType.DMA((2 * pieces + 2 * blocks + 1 + len(kept),))],
        compiler_params=roomy,
        cost_estimate=cost(7),
    )(at, *toks, *weights)
    out_mate = summed(outs[:pieces])
    back_mate = exchange(out_mate).reshape(slots, width)
    out_own = summed(outs[pieces:])

    cots = [in_hbm(x) for x in double_pair(after(recv_cot, out_mate))]
    c_buffers = [pltpu.VMEM(x.shape, BF16) for x in cots]
    unit_rows = ((2 * slots, units), BF16)
    dgate, dup = pl.pallas_call(
        functools.partial(backward_kernel, pieces, step),
        out_shape=[pltpu.HBM(*unit_rows)] * 2,
        in_specs=[SMEM] + [HBM] * (pieces + 3),
        out_specs=[HBM] * 2,
        scratch_shapes=c_buffers
        + [weight_buffer]
        + [pltpu.VMEM(*unit_rows)] * 4
        + [pltpu.SemaphoreType.DMA((pieces + blocks + 4,))],
        compiler_params=roomy,
        cost_estimate=cost(4),
    )(at, *cots, weights[2], in_hbm(keep_gate), in_hbm(keep_up))

    mix_mate = mixed_rows(about_mate, after(back_mate, dgate))
    mix_far = to_mate(mix_mate)

    def grads(lefts, xs, joined):
        count, lanes = len(lefts), 2 * span if joined else span
        return pl.pallas_call(
            functools.partial(grads_kernel, joined, pieces, count, span, 512),
            out_shape=[pltpu.HBM((units, features), BF16)] * count,
            in_specs=[SMEM] + [HBM] * (len(xs) + count),
            out_specs=[HBM] * count,
            scratch_shapes=[pltpu.VMEM(*unit_rows)] * count
            + [pltpu.VMEM((slots, lanes), BF16) for x in xs]
            + [
                pltpu.VMEM((units, 2 * slots), BF16),
                pltpu.VMEM((2, units, 512), BF16),
                pltpu.SemaphoreType.DMA((count + len(xs),)),
                pltpu.SemaphoreType.DMA((2,)),
            ],
            compiler_params=roomy,
            cost_estimate=cost(4 * count),
        )(at, *[in_hbm(x) for x in lefts], *xs)

    (grad_down,) = grads([hidden], cots, True)
    grad_gate, grad_up = grads([dgate, dup], toks, False)
    back_own = exchange(after(out_own, mix_mate)).reshape(slots, width)
    mixed = mixed_rows(about, back_own, mix_far)
    return (
        mixed,
        grad_gate[None],
        grad_up[None],
        grad_down[None],
    )


def solution(mesh):
    in_specs = (
        P("dp", None),
        P("dp", None),
        P("dp", None),
        P("dp", None),
        P("dp"),
        P(),
        P("dp", "tensor", None),
        P("dp", "tensor", None),
        P("dp", "tensor", None),
    )
    out_specs = (
        P("dp", "tensor"),
        P("dp", "tensor", None),
        P("dp", "tensor", None),
        P("dp", "tensor", None),
    )
    return jax.shard_map(body, mesh=mesh, in_specs=in_specs, out_specs=out_specs, check_vma=False)
```

```python
import functools

import jax
import jax.numpy as jnp
from jax import lax
from jax.experimental import pallas as pl
from jax.experimental.pallas import tpu as pltpu
from jax.sharding import PartitionSpec as P

F32 = jnp.float32
BF16 = jnp.bfloat16
LANES = 128
FACTS = 16
VMEM = pl.BlockSpec(memory_space=pltpu.VMEM)
SMEM = pl.BlockSpec(memory_space=pltpu.SMEM)
ANY = pl.BlockSpec(memory_space=pl.ANY)
HBM = pl.BlockSpec(memory_space=pltpu.HBM)


def cost(micros):
    return pl.CostEstimate(
        flops=int(micros * 1e9), bytes_accessed=int(micros * 3e6), transcendentals=0
    )


def in_hbm(value):
    return pltpu.with_memory_space_constraint(value, pltpu.HBM)


def dot(a, b, dims):
    return lax.dot_general(a, b, (dims, ((), ())), preferred_element_type=F32)


def facts_kernel(top, seq_len, place_ref, lengths_ref, ids_ref, weight_ref, forget_ref, out_ref):
    toks = ids_ref.shape[1]
    weight = weight_ref[...]
    out_ref[:top, :] = ids_ref[...].astype(F32)
    out_ref[top : 2 * top, :] = weight / jnp.sum(weight, axis=0, keepdims=True)
    token = place_ref[0] + lax.broadcasted_iota(jnp.int32, (1, toks), 1)
    valid = jnp.zeros((1, toks), jnp.int32)
    for s in range(lengths_ref.shape[0]):
        begin = s * seq_len
        inside = (token >= begin) & (token < begin + lengths_ref[s])
        valid = jnp.where(inside, 1, valid)
    forget = valid * forget_ref[...]
    out_ref[2 * top : 2 * top + 1, :] = (valid - forget).astype(F32)
    out_ref[2 * top + 1 : 2 * top + 2, :] = forget.astype(F32)
    rest = 2 * top + 2
    out_ref[rest:, :] = jnp.zeros((out_ref.shape[0] - rest, toks), F32)


def slot_tables(top, half, capacity, first, info, pick_ref, weighted_ref=None, factor=None):
    toks = info.shape[1]
    expert = (first + lax.broadcasted_iota(jnp.int32, (half, toks), 0)).astype(F32)
    named = jnp.zeros((half, toks), F32)
    weight = jnp.zeros((half, toks), F32)
    for k in range(top):
        hit = info[k : k + 1, :] == expert
        named = jnp.where(hit, 1.0, named)
        weight = jnp.where(hit, info[top + k : top + k + 1, :], weight)
    row = lax.broadcasted_iota(jnp.int32, (toks, toks), 0)
    column = lax.broadcasted_iota(jnp.int32, (toks, toks), 1)
    earlier = jnp.where(row < column, 1.0, 0.0).astype(BF16)
    rank = dot(named.astype(BF16), earlier, ((1,), (0,)))
    rank = jnp.where(named > 0.0, rank, -1.0)
    if factor is not None:
        weight = factor * weight
    slot = lax.broadcasted_iota(jnp.int32, (capacity, toks), 0).astype(F32)
    for e in range(half):
        at = rank[e : e + 1, :] == slot
        rows = slice(e * capacity, (e + 1) * capacity)
        pick_ref[rows, :] = jnp.where(at, 1.0, 0.0)
        if weighted_ref is not None:
            weighted_ref[rows, :] = jnp.where(at, weight[e : e + 1, :], 0.0)


def gather_kernel(top, half, capacity, first_ref, info_ref, x_ref, out_ref, pick_ref, weight_ref):
    info = info_ref[...]
    width = x_ref.shape[1]
    slot_tables(top, half, capacity, first_ref[0], info, pick_ref, weight_ref)
    pick = pick_ref[...]
    out_ref[:, :width] = dot(pick.astype(BF16), x_ref[...], ((1,), (0,))).astype(BF16)
    share = jnp.sum(weight_ref[...], axis=1, keepdims=True)
    high = share.astype(BF16).astype(F32)
    middle = (share - high).astype(BF16).astype(F32)
    flags = info[2 * top : 2 * top + 2, :]
    marks = [jnp.sum(pick * flags[i : i + 1, :], axis=1, keepdims=True) for i in range(2)]
    counts = jnp.sum(flags, axis=1, keepdims=True)
    lane = lax.broadcasted_iota(jnp.int32, (out_ref.shape[0], LANES), 1)
    facts = jnp.zeros((out_ref.shape[0], LANES), F32)
    columns = [high, middle, share - high - middle, marks[0], marks[1], counts[0:1, :], counts[1:2, :]]
    for i, column in enumerate(columns):
        facts = jnp.where(lane == i, column, facts)
    out_ref[:, width:] = facts.astype(BF16)


def cot_kernel(top, half, capacity, first_ref, info_ref, info2_ref, x_ref, x2_ref, out_ref, pick_ref):
    width = x_ref.shape[1]
    for i, (facts, x) in enumerate(((info_ref, x_ref), (info2_ref, x2_ref))):
        slot_tables(top, half, capacity, first_ref[0], facts[...], pick_ref)
        rows = dot(pick_ref[...].astype(BF16), x[...], ((1,), (0,)))
        out_ref[:, i * width : (i + 1) * width] = rows.astype(BF16)


def mix_kernel(top, half, capacity, first_ref, info_ref, back_ref, *rest):
    far_refs, (out_ref, pick_ref, weight_ref) = rest[:-3], rest[-3:]
    slot_tables(top, half, capacity, first_ref[0], info_ref[...], pick_ref, weight_ref)
    weight = weight_ref[...]
    high = weight.astype(BF16)
    low = (weight - high.astype(F32)).astype(BF16)
    back = back_ref[...]
    total = dot(high, back, ((0,), (0,))) + dot(low, back, ((0,), (0,)))
    for far in far_refs:
        total = total + far[...].astype(F32)
    out_ref[...] = total.astype(BF16)


def halve_kernel(core_ref, x_ref, out_ref):
    width = out_ref.shape[1]
    out_ref[...] = x_ref[:, pl.ds(pl.multiple_of(core_ref[0] * width, LANES), width)]


def add_kernel(a_ref, b_ref, out_ref):
    out_ref[...] = (a_ref[...].astype(F32) + b_ref[...].astype(F32)).astype(BF16)


def spans_of(at_ref, first, count, width):
    return [pl.ds(pl.multiple_of(at_ref[first + i], LANES), width) for i in range(count)]


def copier(sems):
    started = []

    def copy(src, dst):
        started.append(pltpu.make_async_copy(src, dst, sems.at[len(started)]))
        started[-1].start()
        return started[-1]

    return copy


def block(ref, j, step):
    return ref.at[pl.ds(j * step, step)]


def stacked(copy, srcs, dst, begin=0):
    slots, width = dst.shape[0] // 2, dst.shape[1]
    if len(srcs) == 1:
        views = [srcs[0].at[:, pl.ds(i * width, width)] for i in range(2)]
    else:
        views = [src.at[:, pl.ds(begin, width)] for src in srcs]
    return [copy(view, block(dst, i, slots)) for i, view in enumerate(views)]


def forward_kernel(pieces, out_pieces, step, at_ref, *refs):
    n = pieces
    xs_in, weights_in, refs = refs[: 2 * n], refs[2 * n : 2 * n + 3], refs[2 * n + 3 :]
    outs, refs = refs[: 3 + 2 * out_pieces], refs[3 + 2 * out_pieces :]
    xs, (gate_w, up_w, down_w), refs = refs[:n], refs[n : n + 3], refs[n + 3 :]
    (keep_gate, keep_up, hidden_ref), own, sems = refs[:3], refs[3:-1], refs[-1]
    copy = copier(sems)
    slots, width = own[0].shape
    spans = spans_of(at_ref, 0, n, xs[0].shape[1])
    out_spans = spans_of(at_ref, n, out_pieces, width)
    blocks = gate_w.shape[0] // step
    x_copies = [started for i, dst in enumerate(xs) for started in stacked(copy, xs_in[i::n], dst)]
    gate_copies, up_copies = [], []
    for j in range(blocks):
        gate_copies.append(copy(block(weights_in[0], j, step), block(gate_w, j, step)))
        up_copies.append(copy(block(weights_in[1], j, step), block(up_w, j, step)))
    down_copy = copy(weights_in[2], down_w)
    for started in x_copies:
        started.wait()
    for j in range(blocks):
        gate_copies[j].wait()
        up_copies[j].wait()
        units = slice(j * step, (j + 1) * step)
        gate = sum(dot(x[...], gate_w[units, span], ((1,), (1,))) for x, span in zip(xs, spans))
        up = sum(dot(x[...], up_w[units, span], ((1,), (1,))) for x, span in zip(xs, spans))
        s = jax.nn.sigmoid(gate)
        silu = gate * s
        keep_gate[:, units] = (up * s * (1.0 + gate * (1.0 - s))).astype(BF16)
        keep_up[:, units] = silu.astype(BF16)
        hidden_ref[:, units] = (silu * up).astype(BF16)
    out_copies = [copy(src, dst) for src, dst in zip((keep_gate, keep_up, hidden_ref), outs[:3])]
    down_copy.wait()
    for i in reversed(range(out_pieces)):
        both = dot(hidden_ref[...], down_w[:, out_spans[i]], ((1,), (0,))).astype(BF16)
        own[i][...] = both[:slots]
        out_copies.append(copy(own[i], outs[3 + out_pieces + i]))
        outs[3 + i][...] = both[slots:]
    for started in out_copies:
        started.wait()


def gradients_kernel(pieces, cot_pieces, capacity, scale, step, at_ref, *refs):
    n, m = pieces, cot_pieces
    cots_in, toks_in, refs = refs[:m], refs[m : m + 2 * n], refs[m + 2 * n :]
    rows_in, inputs, refs = refs[:2], refs[2:6], refs[6:]
    outs, cots, toks, refs = refs[:3], refs[3 : 3 + m], refs[3 + m : 3 + m + n], refs[3 + m + n :]
    down_w, keep_gate, keep_up, hidden, dgate, dup, facts_ref, turned, held, sems = refs
    copy = copier(sems)
    spans = spans_of(at_ref, 0, n, toks[0].shape[1])
    spans = spans_of(at_ref, n, m, cots[0].shape[1])
    facts_copies = stacked(copy, rows_in, facts_ref, rows_in[0].shape[1] - LANES)
    hidden_copy = copy(inputs[3], hidden)
    cot_copies = [stacked(copy, [src], dst) for src, dst in zip(cots_in, cots)]
    down_copy = copy(inputs[0], down_w)
    keep_copies = [copy(inputs[1], keep_gate), copy(inputs[2], keep_up)]
    tok_copies = [stacked(copy, toks_in[i::n], dst) for i, dst in enumerate(toks)]
    for started in facts_copies:
        started.wait()
    facts = facts_ref[...].astype(F32)
    total = jnp.zeros((1, LANES), F32)
    for row in range(0, facts.shape[0], capacity):
        total = total + facts[row : row + 1, :]
    coefficient = scale * (facts[:, 3:4] / total[:, 5:6] - facts[:, 4:5] / total[:, 6:7])
    slot_weight = coefficient * (facts[:, 0:1] + facts[:, 1:2] + facts[:, 2:3])
    for i in range(m):
        for started in cot_copies[i]:
            started.wait()
        cots[i][...] = (slot_weight * cots[i][...].astype(F32)).astype(BF16)
    done = [[] for _ in range(max(n, m))]
    written = []

    def outer(left, xs, spans, copies, k):
        turned[...] = left[...].T
        for i, (x, span) in enumerate(zip(xs, spans)):
            for started in copies[i]:
                started.wait()
            width = x.shape[1]
            place = slice(i * width, (i + 1) * width)
            held[k, :, place] = dot(turned[...], x[...], ((1,), (0,))).astype(BF16)
            written.append(copy(held.at[k, :, pl.ds(i * width, width)], outs[k].at[:, span]))

    hidden_copy.wait()
    outer(hidden, cots, spans, done, 2)
    down_copy.wait()
    for started in keep_copies:
        started.wait()
    for begin in range(0, down_w.shape[0], step):
        units = slice(begin, begin + step)
        dhidden = sum(dot(x[...], down_w[units, span], ((1,), (1,))) for x, span in zip(cots, spans))
        dgate[:, units] = (dhidden * keep_gate[:, units].astype(F32)).astype(BF16)
        dup[:, units] = (dhidden * keep_up[:, units].astype(F32)).astype(BF16)
    outer(dgate, toks, spans, tok_copies, 0)
    outer(dup, toks, spans, done, 1)
    for started in written:
        started.wait()


def body(
    tokens,
    cotangent,
    expert_ids,
    route_weight,
    forget_mask,
    lengths,
    gate_weight,
    up_weight,
    down_weight,
):
    tok_rows, features = tokens.shape
    top = expert_ids.shape[1]
    owners = lax.axis_size("dp")
    parts = lax.axis_size("tensor")
    half = owners // 2
    width = features // parts
    capacity = 5 * tok_rows * top // (4 * owners)
    slots = half * capacity
    seq_len = tok_rows * owners // lengths.shape[0]
    me = lax.axis_index("dp")
    core = lax.axis_index("tensor")
    mates = [(i, (i + half) % owners) for i in range(owners)]
    halves = [list(range(half)), list(range(half, owners))]
    first = ((me // half) * half).astype(jnp.int32).reshape(1)
    place = (me * tok_rows).astype(jnp.int32).reshape(1)
    shape = jax.ShapeDtypeStruct
    table = pltpu.VMEM((slots, tok_rows), F32)
    limit = pltpu.CompilerParams(vmem_limit_bytes=8 * 2**20)

    def to_mate(value):
        return lax.ppermute(value, "dp", mates)

    def exchange(value):
        value = value.reshape(half, value.shape[0] // half, value.shape[1])
        return lax.all_to_all(
            value, "dp", split_axis=0, concat_axis=0, axis_index_groups=halves, tiled=True
        )

    def swapped(value):
        return lax.ppermute(value, "tensor", [(0, 1), (1, 0)])

    def my_features(value, micros):
        return pl.pallas_call(
            halve_kernel,
            out_shape=shape((tok_rows, width), BF16),
            in_specs=[SMEM, VMEM],
            out_specs=VMEM,
            compiler_params=limit,
            cost_estimate=cost(micros),
        )(core.astype(jnp.int32).reshape(1), value)

    def after(value, *others):
        return lax.optimization_barrier((value, *others))[0]

    def mixed_rows(info, back, *far):
        return pl.pallas_call(
            functools.partial(mix_kernel, top, half, capacity),
            out_shape=jax.ShapeDtypeStruct((tok_rows, width), BF16),
            in_specs=[SMEM, VMEM, VMEM] + [VMEM] * len(far),
            out_specs=VMEM,
            scratch_shapes=[table, table],
            compiler_params=limit,
            cost_estimate=cost(1),
        )(first, info, back, *far)

    tok_mine = my_features(tokens, 1)
    tok_mate = to_mate(tok_mine)
    expert_ids = after(expert_ids, tok_mine)
    about = pl.pallas_call(
        functools.partial(facts_kernel, top, seq_len),
        out_shape=jax.ShapeDtypeStruct((FACTS, tok_rows), F32),
        in_specs=[SMEM, SMEM, VMEM, VMEM, VMEM],
        out_specs=VMEM,
        compiler_params=limit,
        cost_estimate=cost(1),
    )(place, lengths, expert_ids.T, route_weight.T, forget_mask.reshape(1, tok_rows))
    about_mate = to_mate(about)

    def gathered(info, x, micros):
        return pl.pallas_call(
            functools.partial(gather_kernel, top, half, capacity),
            out_shape=shape((slots, width + LANES), BF16),
            in_specs=[SMEM, VMEM, VMEM],
            out_specs=VMEM,
            scratch_shapes=[table, table],
            compiler_params=limit,
            cost_estimate=cost(micros),
        )(first, info, x)

    recv_own = exchange(gathered(about, tok_mine, 1)).reshape(slots, width + LANES)
    send_mate = gathered(about_mate, tok_mate, 20)
    recv_mate = exchange(after(send_mate, recv_own)).reshape(slots, width + LANES)

    cot_mine = my_features(after(cotangent, about), 1)
    cot_mate = to_mate(after(cot_mine, tok_mate))
    send_cot = pl.pallas_call(
        functools.partial(cot_kernel, top, half, capacity),
        out_shape=shape((slots, 2 * width), BF16),
        in_specs=[SMEM] + [VMEM] * 4,
        out_specs=VMEM,
        scratch_shapes=[table],
        compiler_params=limit,
        cost_estimate=cost(15),
    )(first, about, about_mate, cot_mine, cot_mate)
    recv_own, recv_mate = after(recv_own, send_cot), after(recv_mate, send_cot)
    recv_cot = exchange(after(send_cot, recv_mate)).reshape(slots, 2 * width)

    gate_w, up_w, down_w = gate_weight[0], up_weight[0], down_weight[0]
    weights = [in_hbm(w) for w in (gate_w, up_w, down_w)]
    units = gate_w.shape[0]
    step = min(units, 256)
    blocks = units // step

    def all_features(row):
        return lax.all_gather(row, "tensor", axis=1, tiled=True)

    if parts == 2:
        other_own = swapped(recv_own)
        toks = [recv_own, other_own, recv_mate, swapped(after(recv_mate, other_own))]
        starts = [core * width, (1 - core) * width] * 2
        span = width
    else:
        toks = [all_features(recv_own[:, :width]), all_features(recv_mate[:, :width])]
        starts = [core * 0] * 2
        span = features
    at = jnp.stack(starts).astype(jnp.int32)
    toks = [in_hbm(x) for x in toks]
    n = m = len(toks) // 2
    weight_buffer = pltpu.VMEM((units, features), BF16)
    unit_rows = ((2 * slots, units), BF16)
    tok_buffers = [pltpu.VMEM((2 * slots, span), BF16)] * n
    cot_buffers = [pltpu.VMEM((2 * slots, span), BF16)] * m
    roomy = pltpu.CompilerParams(vmem_limit_bytes=36 * 2**20)

    def summed(outs):
        if parts != 2:
            return lax.psum_scatter(outs[0], "tensor", scatter_dimension=1, tiled=True)
        return pl.pallas_call(
            add_kernel,
            out_shape=shape((slots, width), BF16),
            in_specs=[VMEM] * 2,
            out_specs=VMEM,
            compiler_params=limit,
            cost_estimate=cost(1),
        )(outs[0], swapped(outs[1]))

    piece = (slots, span)
    keep_gate, keep_up, hidden, *outs = pl.pallas_call(
        functools.partial(forward_kernel, n, m, step),
        out_shape=[pltpu.HBM(*unit_rows)] * 3
        + [shape(piece, BF16)] * m
        + [pltpu.HBM(piece, BF16)] * m,
        in_specs=[SMEM] + [HBM] * (2 * n + 3),
        out_specs=[HBM] * 3 + [VMEM] * m + [HBM] * m,
        scratch_shapes=tok_buffers
        + [weight_buffer] * 3
        + [pltpu.VMEM(*unit_rows)] * 3
        + [pltpu.VMEM(piece, BF16)] * m
        + [pltpu.SemaphoreType.DMA((2 * n + 2 * blocks + 4 + m,))],
        compiler_params=roomy,
        cost_estimate=cost(8),
    )(at, *toks, *weights)
    out_mate = summed(outs[:m])
    back_mate = exchange(out_mate).reshape(slots, width)
    out_own = summed(outs[m:])

    recv_cot = after(recv_cot, out_mate)
    if parts == 2:
        cots = [recv_cot, swapped(recv_cot)]
    else:
        both = [all_features(recv_cot[:, :width]), all_features(recv_cot[:, width:])]
        cots = [jnp.concatenate(both, axis=1)]
    mix_mate = mixed_rows(about_mate, back_mate)
    mix_far = to_mate(mix_mate)
    keeps = [in_hbm(x) for x in (keep_gate, keep_up, after(hidden, mix_mate))]
    grad_gate, grad_up, grad_down = pl.pallas_call(
        functools.partial(gradients_kernel, n, m, capacity, float(top * tok_rows), step),
        out_shape=[pltpu.HBM((units, features), BF16)] * 3,
        in_specs=[SMEM] + [HBM] * (2 * n + m + 6),
        out_specs=[HBM] * 3,
        scratch_shapes=cot_buffers
        + tok_buffers
        + [weight_buffer]
        + [pltpu.VMEM(*unit_rows)] * 5
        + [
            pltpu.VMEM((2 * slots, LANES), BF16),
            pltpu.VMEM((units, 2 * slots), BF16),
            pltpu.VMEM((3, units, features), BF16),
            pltpu.SemaphoreType.DMA((4 * n + 3 * m + 6,)),
        ],
        compiler_params=roomy,
        cost_estimate=cost(20),
    )(at, *[in_hbm(x) for x in cots], *toks, in_hbm(recv_own), in_hbm(recv_mate), weights[2], *keeps)
    back_own = exchange(after(out_own, mix_mate)).reshape(slots, width)
    mixed = mixed_rows(about, back_own, mix_far)
    return (
        mixed,
        grad_gate[None],
        grad_up[None],
        grad_down[None],
    )


def solution(mesh):
    in_specs = (
        P("dp", None),
        P("dp", None),
        P("dp", None),
        P("dp", None),
        P("dp"),
        P(),
        P("dp", "tensor", None),
        P("dp", "tensor", None),
        P("dp", "tensor", None),
    )
    out_specs = (
        P("dp", "tensor"),
        P("dp", "tensor", None),
        P("dp", "tensor", None),
        P("dp", "tensor", None),
    )
    return jax.shard_map(body, mesh=mesh, in_specs=in_specs, out_specs=out_specs, check_vma=False)
```

```python
import functools

import jax
import jax.numpy as jnp
from jax import lax
from jax.experimental import pallas as pl
from jax.experimental.pallas import tpu as pltpu
from jax.sharding import PartitionSpec as P

F32 = jnp.float32
BF16 = jnp.bfloat16
LANES = 128
FACTS = 16
VMEM = pl.BlockSpec(memory_space=pltpu.VMEM)
SMEM = pl.BlockSpec(memory_space=pltpu.SMEM)
ANY = pl.BlockSpec(memory_space=pl.ANY)
HBM = pl.BlockSpec(memory_space=pltpu.HBM)


def cost(micros):
    return pl.CostEstimate(
        flops=int(micros * 1e9), bytes_accessed=int(micros * 3e6), transcendentals=0
    )


def in_hbm(value):
    return pltpu.with_memory_space_constraint(value, pltpu.HBM)


def dot(a, b, dims):
    return lax.dot_general(a, b, (dims, ((), ())), preferred_element_type=F32)


def facts_kernel(top, seq_len, place_ref, lengths_ref, ids_ref, weight_ref, forget_ref, out_ref):
    toks = ids_ref.shape[1]
    weight = weight_ref[...]
    out_ref[:top, :] = ids_ref[...].astype(F32)
    out_ref[top : 2 * top, :] = weight / jnp.sum(weight, axis=0, keepdims=True)
    token = place_ref[0] + lax.broadcasted_iota(jnp.int32, (1, toks), 1)
    valid = jnp.zeros((1, toks), jnp.int32)
    for s in range(lengths_ref.shape[0]):
        begin = s * seq_len
        inside = (token >= begin) & (token < begin + lengths_ref[s])
        valid = jnp.where(inside, 1, valid)
    forget = valid * forget_ref[...]
    out_ref[2 * top : 2 * top + 1, :] = (valid - forget).astype(F32)
    out_ref[2 * top + 1 : 2 * top + 2, :] = forget.astype(F32)
    rest = 2 * top + 2
    out_ref[rest:, :] = jnp.zeros((out_ref.shape[0] - rest, toks), F32)


def slot_tables(top, half, capacity, first, info, pick_ref, weighted_ref=None, factor=None):
    toks = info.shape[1]
    expert = (first + lax.broadcasted_iota(jnp.int32, (half, toks), 0)).astype(F32)
    named = jnp.zeros((half, toks), F32)
    weight = jnp.zeros((half, toks), F32)
    for k in range(top):
        hit = info[k : k + 1, :] == expert
        named = jnp.where(hit, 1.0, named)
        weight = jnp.where(hit, info[top + k : top + k + 1, :], weight)
    row = lax.broadcasted_iota(jnp.int32, (toks, toks), 0)
    column = lax.broadcasted_iota(jnp.int32, (toks, toks), 1)
    earlier = jnp.where(row < column, 1.0, 0.0).astype(BF16)
    rank = dot(named.astype(BF16), earlier, ((1,), (0,)))
    rank = jnp.where(named > 0.0, rank, -1.0)
    if factor is not None:
        weight = factor * weight
    slot = lax.broadcasted_iota(jnp.int32, (capacity, toks), 0).astype(F32)
    for e in range(half):
        at = rank[e : e + 1, :] == slot
        rows = slice(e * capacity, (e + 1) * capacity)
        pick_ref[rows, :] = jnp.where(at, 1.0, 0.0)
        if weighted_ref is not None:
            weighted_ref[rows, :] = jnp.where(at, weight[e : e + 1, :], 0.0)


def gather_kernel(top, half, capacity, first_ref, info_ref, x_ref, out_ref, pick_ref):
    slot_tables(top, half, capacity, first_ref[0], info_ref[...], pick_ref)
    out_ref[...] = dot(pick_ref[...].astype(BF16), x_ref[...], ((1,), (0,))).astype(BF16)


def cot_kernel(top, half, capacity, first_ref, info_ref, info2_ref, x_ref, x2_ref, out_ref, pick_ref, weight_ref):
    width = x_ref.shape[1]
    lane = lax.broadcasted_iota(jnp.int32, (out_ref.shape[0], LANES), 1)
    facts = jnp.zeros((out_ref.shape[0], LANES), F32)
    for i, (info_in, x) in enumerate(((info_ref, x_ref), (info2_ref, x2_ref))):
        info = info_in[...]
        slot_tables(top, half, capacity, first_ref[0], info, pick_ref, weight_ref)
        pick = pick_ref[...]
        rows = dot(pick.astype(BF16), x[...], ((1,), (0,)))
        out_ref[:, i * width : (i + 1) * width] = rows.astype(BF16)
        share = jnp.sum(weight_ref[...], axis=1, keepdims=True)
        high = share.astype(BF16).astype(F32)
        middle = (share - high).astype(BF16).astype(F32)
        flags = info[2 * top : 2 * top + 2, :]
        marks = [jnp.sum(pick * flags[k : k + 1, :], axis=1, keepdims=True) for k in range(2)]
        counts = jnp.sum(flags, axis=1, keepdims=True)
        columns = [high, middle, share - high - middle, marks[0], marks[1], counts[0:1, :], counts[1:2, :]]
        for k, column in enumerate(columns):
            facts = jnp.where(lane == i * LANES // 2 + k, column, facts)
    out_ref[:, 2 * width :] = facts.astype(BF16)


def mix_kernel(top, half, capacity, first_ref, info_ref, back_ref, *rest):
    far_refs, (out_ref, pick_ref, weight_ref) = rest[:-3], rest[-3:]
    slot_tables(top, half, capacity, first_ref[0], info_ref[...], pick_ref, weight_ref)
    weight = weight_ref[...]
    high = weight.astype(BF16)
    low = (weight - high.astype(F32)).astype(BF16)
    back = back_ref[...]
    total = dot(high, back, ((0,), (0,))) + dot(low, back, ((0,), (0,)))
    for far in far_refs:
        total = total + far[...].astype(F32)
    out_ref[...] = total.astype(BF16)


def halve_kernel(core_ref, x_ref, out_ref, sem):
    width = out_ref.shape[1]
    mine = pl.ds(pl.multiple_of(core_ref[0] * width, LANES), width)
    copy = pltpu.make_async_copy(x_ref.at[:, mine], out_ref, sem)
    copy.start()
    copy.wait()


def add_kernel(a_ref, b_ref, out_ref):
    out_ref[...] = (a_ref[...].astype(F32) + b_ref[...].astype(F32)).astype(BF16)


def spans_of(at_ref, first, count, width):
    return [pl.ds(pl.multiple_of(at_ref[first + i], LANES), width) for i in range(count)]


def copier(sems):
    started = []

    def copy(src, dst):
        started.append(pltpu.make_async_copy(src, dst, sems.at[len(started)]))
        started[-1].start()
        return started[-1]

    return copy


def block(ref, j, step):
    return ref.at[pl.ds(j * step, step)]


def stacked(copy, srcs, dst, begin=0):
    slots, width = dst.shape[0] // 2, dst.shape[1]
    if len(srcs) == 1:
        views = [srcs[0].at[:, pl.ds(i * width, width)] for i in range(2)]
    else:
        views = [src.at[:, pl.ds(begin, width)] for src in srcs]
    return [copy(view, block(dst, i, slots)) for i, view in enumerate(views)]


def forward_kernel(pieces, out_pieces, step, at_ref, *refs):
    n = pieces
    xs_in, weights_in, refs = refs[: 2 * n], refs[2 * n : 2 * n + 3], refs[2 * n + 3 :]
    outs, refs = refs[: 3 + 2 * out_pieces], refs[3 + 2 * out_pieces :]
    xs, (gate_w, up_w, down_w), refs = refs[:n], refs[n : n + 3], refs[n + 3 :]
    (keep_gate, keep_up, hidden_ref), own, sems = refs[:3], refs[3:-1], refs[-1]
    copy = copier(sems)
    slots, width = own[0].shape
    spans = spans_of(at_ref, 0, n, xs[0].shape[1])
    out_spans = spans_of(at_ref, n, out_pieces, width)
    blocks = gate_w.shape[0] // step
    x_copies = [started for i, dst in enumerate(xs) for started in stacked(copy, xs_in[i::n], dst)]
    gate_copies, up_copies = [], []
    for j in range(blocks):
        gate_copies.append(copy(block(weights_in[0], j, step), block(gate_w, j, step)))
        up_copies.append(copy(block(weights_in[1], j, step), block(up_w, j, step)))
    down_copy = copy(weights_in[2], down_w)
    for started in x_copies:
        started.wait()
    for j in range(blocks):
        gate_copies[j].wait()
        up_copies[j].wait()
        units = slice(j * step, (j + 1) * step)
        gate = sum(dot(x[...], gate_w[units, span], ((1,), (1,))) for x, span in zip(xs, spans))
        up = sum(dot(x[...], up_w[units, span], ((1,), (1,))) for x, span in zip(xs, spans))
        s = jax.nn.sigmoid(gate)
        silu = gate * s
        keep_gate[:, units] = (up * s * (1.0 + gate * (1.0 - s))).astype(BF16)
        keep_up[:, units] = silu.astype(BF16)
        hidden_ref[:, units] = (silu * up).astype(BF16)
    out_copies = [copy(src, dst) for src, dst in zip((keep_gate, keep_up, hidden_ref), outs[:3])]
    down_copy.wait()
    for i in reversed(range(out_pieces)):
        both = dot(hidden_ref[...], down_w[:, out_spans[i]], ((1,), (0,))).astype(BF16)
        own[i][...] = both[:slots]
        out_copies.append(copy(own[i], outs[3 + out_pieces + i]))
        outs[3 + i][...] = both[slots:]
    for started in out_copies:
        started.wait()


def gradients_kernel(pieces, cot_pieces, capacity, scale, step, at_ref, *refs):
    n, m = pieces, cot_pieces
    cots_in, toks_in, refs = refs[:m], refs[m : m + 2 * n], refs[m + 2 * n :]
    facts_in, inputs, refs = refs[0], refs[1:5], refs[5:]
    outs, cots, toks, refs = refs[:3], refs[3 : 3 + m], refs[3 + m : 3 + m + n], refs[3 + m + n :]
    down_w, keep_gate, keep_up, hidden, dgate, dup, facts_ref, turned, held, sems = refs
    copy = copier(sems)
    spans = spans_of(at_ref, 0, n, toks[0].shape[1])
    spans = spans_of(at_ref, n, m, cots[0].shape[1])
    facts_copy = copy(facts_in.at[:, pl.ds(facts_in.shape[1] - LANES, LANES)], facts_ref)
    hidden_copy = copy(inputs[3], hidden)
    cot_copies = [stacked(copy, [src], dst) for src, dst in zip(cots_in, cots)]
    down_copy = copy(inputs[0], down_w)
    keep_copies = [copy(inputs[1], keep_gate), copy(inputs[2], keep_up)]
    tok_copies = [stacked(copy, toks_in[i::n], dst) for i, dst in enumerate(toks)]
    facts_copy.wait()
    facts = facts_ref[...].astype(F32)
    slots, side = facts.shape[0], LANES // 2
    total = jnp.zeros((1, LANES), F32)
    for row in range(0, slots, capacity):
        total = total + facts[row : row + 1, :]
    retain_all = total[:, 5:6] + total[:, side + 5 : side + 6]
    forget_all = total[:, 6:7] + total[:, side + 6 : side + 7]

    def weight_of(begin):
        share, retain, forget = facts[:, begin : begin + 3], facts[:, begin + 3 : begin + 4], facts[:, begin + 4 : begin + 5]
        coefficient = scale * (retain / retain_all - forget / forget_all)
        return coefficient * (share[:, 0:1] + share[:, 1:2] + share[:, 2:3])

    slot_weights = [weight_of(0), weight_of(side)]
    for i in range(m):
        for started in cot_copies[i]:
            started.wait()
        for part in range(2):
            rows = slice(part * slots, (part + 1) * slots)
            cots[i][rows, :] = (slot_weights[part] * cots[i][rows, :].astype(F32)).astype(BF16)
    done = [[] for _ in range(max(n, m))]
    written = []

    def outer(left, xs, spans, copies, k):
        turned[...] = left[...].T
        for i, (x, span) in enumerate(zip(xs, spans)):
            for started in copies[i]:
                started.wait()
            width = x.shape[1]
            place = slice(i * width, (i + 1) * width)
            held[k, :, place] = dot(turned[...], x[...], ((1,), (0,))).astype(BF16)
            written.append(copy(held.at[k, :, pl.ds(i * width, width)], outs[k].at[:, span]))

    hidden_copy.wait()
    outer(hidden, cots, spans, done, 2)
    down_copy.wait()
    for started in keep_copies:
        started.wait()
    for begin in range(0, down_w.shape[0], step):
        units = slice(begin, begin + step)
        dhidden = sum(dot(x[...], down_w[units, span], ((1,), (1,))) for x, span in zip(cots, spans))
        dgate[:, units] = (dhidden * keep_gate[:, units].astype(F32)).astype(BF16)
        dup[:, units] = (dhidden * keep_up[:, units].astype(F32)).astype(BF16)
    outer(dgate, toks, spans, tok_copies, 0)
    outer(dup, toks, spans, done, 1)
    for started in written:
        started.wait()


def body(
    tokens,
    cotangent,
    expert_ids,
    route_weight,
    forget_mask,
    lengths,
    gate_weight,
    up_weight,
    down_weight,
):
    tok_rows, features = tokens.shape
    top = expert_ids.shape[1]
    owners = lax.axis_size("dp")
    parts = lax.axis_size("tensor")
    half = owners // 2
    width = features // parts
    capacity = 5 * tok_rows * top // (4 * owners)
    slots = half * capacity
    seq_len = tok_rows * owners // lengths.shape[0]
    me = lax.axis_index("dp")
    core = lax.axis_index("tensor")
    mates = [(i, (i + half) % owners) for i in range(owners)]
    halves = [list(range(half)), list(range(half, owners))]
    first = ((me // half) * half).astype(jnp.int32).reshape(1)
    place = (me * tok_rows).astype(jnp.int32).reshape(1)
    shape = jax.ShapeDtypeStruct
    table = pltpu.VMEM((slots, tok_rows), F32)
    limit = pltpu.CompilerParams(vmem_limit_bytes=8 * 2**20)

    def to_mate(value):
        return lax.ppermute(value, "dp", mates)

    def exchange(value):
        value = value.reshape(half, value.shape[0] // half, value.shape[1])
        return lax.all_to_all(
            value, "dp", split_axis=0, concat_axis=0, axis_index_groups=halves, tiled=True
        )

    def swapped(value):
        return lax.ppermute(value, "tensor", [(0, 1), (1, 0)])

    def my_features(value, micros):
        return pl.pallas_call(
            halve_kernel,
            out_shape=shape((tok_rows, width), BF16),
            in_specs=[SMEM, HBM],
            out_specs=VMEM,
            scratch_shapes=[pltpu.SemaphoreType.DMA],
            compiler_params=limit,
            cost_estimate=cost(micros),
        )(core.astype(jnp.int32).reshape(1), in_hbm(value))

    def after(value, *others):
        return lax.optimization_barrier((value, *others))[0]

    def mixed_rows(info, back, *far):
        return pl.pallas_call(
            functools.partial(mix_kernel, top, half, capacity),
            out_shape=jax.ShapeDtypeStruct((tok_rows, width), BF16),
            in_specs=[SMEM, VMEM, VMEM] + [VMEM] * len(far),
            out_specs=VMEM,
            scratch_shapes=[table, table],
            compiler_params=limit,
            cost_estimate=cost(1),
        )(first, info, back, *far)

    tok_mine = my_features(tokens, 1)
    tok_mate = to_mate(tok_mine)
    expert_ids = after(expert_ids, tok_mine)
    about = pl.pallas_call(
        functools.partial(facts_kernel, top, seq_len),
        out_shape=jax.ShapeDtypeStruct((FACTS, tok_rows), F32),
        in_specs=[SMEM, SMEM, VMEM, VMEM, VMEM],
        out_specs=VMEM,
        compiler_params=limit,
        cost_estimate=cost(1),
    )(place, lengths, expert_ids.T, route_weight.T, forget_mask.reshape(1, tok_rows))
    about_mate = to_mate(about)

    def gathered(info, x, micros):
        return pl.pallas_call(
            functools.partial(gather_kernel, top, half, capacity),
            out_shape=shape((slots, width), BF16),
            in_specs=[SMEM, VMEM, VMEM],
            out_specs=VMEM,
            scratch_shapes=[table],
            compiler_params=limit,
            cost_estimate=cost(micros),
        )(first, info, x)

    recv_own = exchange(gathered(about, tok_mine, 1)).reshape(slots, width)
    send_mate = gathered(about_mate, tok_mate, 20)
    recv_mate = exchange(after(send_mate, recv_own)).reshape(slots, width)

    cot_mine = my_features(after(cotangent, about), 1)
    cot_mate = to_mate(after(cot_mine, tok_mate))
    send_cot = pl.pallas_call(
        functools.partial(cot_kernel, top, half, capacity),
        out_shape=shape((slots, 2 * width + LANES), BF16),
        in_specs=[SMEM] + [VMEM] * 4,
        out_specs=VMEM,
        scratch_shapes=[table, table],
        compiler_params=limit,
        cost_estimate=cost(15),
    )(first, about, about_mate, cot_mine, cot_mate)
    recv_own, recv_mate = after(recv_own, send_cot), after(recv_mate, send_cot)
    recv_cot = exchange(after(send_cot, recv_mate)).reshape(slots, 2 * width + LANES)

    gate_w, up_w, down_w = gate_weight[0], up_weight[0], down_weight[0]
    weights = [in_hbm(w) for w in (gate_w, up_w, down_w)]
    units = gate_w.shape[0]
    step = min(units, 256)
    blocks = units // step

    def all_features(row):
        return lax.all_gather(row, "tensor", axis=1, tiled=True)

    if parts == 2:
        other_own = swapped(recv_own)
        toks = [recv_own, other_own, recv_mate, swapped(after(recv_mate, other_own))]
        starts = [core * width, (1 - core) * width] * 2
        span = width
    else:
        toks = [all_features(recv_own), all_features(recv_mate)]
        starts = [core * 0] * 2
        span = features
    at = jnp.stack(starts).astype(jnp.int32)
    toks = [in_hbm(x) for x in toks]
    n = m = len(toks) // 2
    weight_buffer = pltpu.VMEM((units, features), BF16)
    unit_rows = ((2 * slots, units), BF16)
    tok_buffers = [pltpu.VMEM((2 * slots, span), BF16)] * n
    cot_buffers = [pltpu.VMEM((2 * slots, span), BF16)] * m
    roomy = pltpu.CompilerParams(vmem_limit_bytes=36 * 2**20)

    def summed(outs):
        if parts != 2:
            return lax.psum_scatter(outs[0], "tensor", scatter_dimension=1, tiled=True)
        return pl.pallas_call(
            add_kernel,
            out_shape=shape((slots, width), BF16),
            in_specs=[VMEM] * 2,
            out_specs=VMEM,
            compiler_params=limit,
            cost_estimate=cost(1),
        )(outs[0], swapped(outs[1]))

    piece = (slots, span)
    keep_gate, keep_up, hidden, *outs = pl.pallas_call(
        functools.partial(forward_kernel, n, m, step),
        out_shape=[pltpu.HBM(*unit_rows)] * 3
        + [shape(piece, BF16)] * m
        + [pltpu.HBM(piece, BF16)] * m,
        in_specs=[SMEM] + [HBM] * (2 * n + 3),
        out_specs=[HBM] * 3 + [VMEM] * m + [HBM] * m,
        scratch_shapes=tok_buffers
        + [weight_buffer] * 3
        + [pltpu.VMEM(*unit_rows)] * 3
        + [pltpu.VMEM(piece, BF16)] * m
        + [pltpu.SemaphoreType.DMA((2 * n + 2 * blocks + 4 + m,))],
        compiler_params=roomy,
        cost_estimate=cost(8),
    )(at, *toks, *weights)
    out_mate = summed(outs[:m])
    back_mate = exchange(out_mate).reshape(slots, width)
    out_own = summed(outs[m:])

    recv_cot = after(recv_cot, out_mate)
    if parts == 2:
        cots = [recv_cot, swapped(recv_cot)]
    else:
        both = [all_features(recv_cot[:, i * width : (i + 1) * width]) for i in range(2)]
        cots = [jnp.concatenate(both, axis=1)]
    mix_mate = mixed_rows(about_mate, back_mate)
    mix_far = to_mate(mix_mate)
    keeps = [in_hbm(x) for x in (keep_gate, keep_up, after(hidden, mix_mate))]
    grad_gate, grad_up, grad_down = pl.pallas_call(
        functools.partial(gradients_kernel, n, m, capacity, float(top * tok_rows), step),
        out_shape=[pltpu.HBM((units, features), BF16)] * 3,
        in_specs=[SMEM] + [HBM] * (2 * n + m + 5),
        out_specs=[HBM] * 3,
        scratch_shapes=cot_buffers
        + tok_buffers
        + [weight_buffer]
        + [pltpu.VMEM(*unit_rows)] * 5
        + [
            pltpu.VMEM((slots, LANES), BF16),
            pltpu.VMEM((units, 2 * slots), BF16),
            pltpu.VMEM((3, units, features), BF16),
            pltpu.SemaphoreType.DMA((4 * n + 3 * m + 5,)),
        ],
        compiler_params=roomy,
        cost_estimate=cost(20),
    )(at, *[in_hbm(x) for x in cots], *toks, in_hbm(recv_cot), weights[2], *keeps)
    back_own = exchange(after(out_own, mix_mate)).reshape(slots, width)
    mixed = mixed_rows(after(about, grad_down), back_own, mix_far)
    return (
        mixed,
        grad_gate[None],
        grad_up[None],
        grad_down[None],
    )


def solution(mesh):
    in_specs = (
        P("dp", None),
        P("dp", None),
        P("dp", None),
        P("dp", None),
        P("dp"),
        P(),
        P("dp", "tensor", None),
        P("dp", "tensor", None),
        P("dp", "tensor", None),
    )
    out_specs = (
        P("dp", "tensor"),
        P("dp", "tensor", None),
        P("dp", "tensor", None),
        P("dp", "tensor", None),
    )
    return jax.shard_map(body, mesh=mesh, in_specs=in_specs, out_specs=out_specs, check_vma=False)
```

```python
import functools

import jax
import jax.numpy as jnp
from jax import lax
from jax.experimental import pallas as pl
from jax.experimental.pallas import tpu as pltpu
from jax.sharding import PartitionSpec as P

F32 = jnp.float32
BF16 = jnp.bfloat16
LANES = 128
FACTS = 16
VMEM = pl.BlockSpec(memory_space=pltpu.VMEM)
SMEM = pl.BlockSpec(memory_space=pltpu.SMEM)
ANY = pl.BlockSpec(memory_space=pl.ANY)
HBM = pl.BlockSpec(memory_space=pltpu.HBM)


def cost(micros):
    return pl.CostEstimate(
        flops=int(micros * 1e9), bytes_accessed=int(micros * 3e6), transcendentals=0
    )


def in_hbm(value):
    return pltpu.with_memory_space_constraint(value, pltpu.HBM)


def dot(a, b, dims):
    return lax.dot_general(a, b, (dims, ((), ())), preferred_element_type=F32)


def facts_kernel(top, seq_len, place_ref, lengths_ref, ids_ref, weight_ref, forget_ref, out_ref):
    toks = ids_ref.shape[1]
    weight = weight_ref[...]
    out_ref[:top, :] = ids_ref[...].astype(F32)
    out_ref[top : 2 * top, :] = weight / jnp.sum(weight, axis=0, keepdims=True)
    token = place_ref[0] + lax.broadcasted_iota(jnp.int32, (1, toks), 1)
    valid = jnp.zeros((1, toks), jnp.int32)
    for s in range(lengths_ref.shape[0]):
        begin = s * seq_len
        inside = (token >= begin) & (token < begin + lengths_ref[s])
        valid = jnp.where(inside, 1, valid)
    forget = valid * forget_ref[...]
    out_ref[2 * top : 2 * top + 1, :] = (valid - forget).astype(F32)
    out_ref[2 * top + 1 : 2 * top + 2, :] = forget.astype(F32)
    rest = 2 * top + 2
    out_ref[rest:, :] = jnp.zeros((out_ref.shape[0] - rest, toks), F32)


def slot_tables(top, half, capacity, first, info, pick_ref, weighted_ref=None, factor=None):
    toks = info.shape[1]
    expert = (first + lax.broadcasted_iota(jnp.int32, (half, toks), 0)).astype(F32)
    named = jnp.zeros((half, toks), F32)
    weight = jnp.zeros((half, toks), F32)
    for k in range(top):
        hit = info[k : k + 1, :] == expert
        named = jnp.where(hit, 1.0, named)
        weight = jnp.where(hit, info[top + k : top + k + 1, :], weight)
    row = lax.broadcasted_iota(jnp.int32, (toks, toks), 0)
    column = lax.broadcasted_iota(jnp.int32, (toks, toks), 1)
    earlier = jnp.where(row < column, 1.0, 0.0).astype(BF16)
    rank = dot(named.astype(BF16), earlier, ((1,), (0,)))
    rank = jnp.where(named > 0.0, rank, -1.0)
    if factor is not None:
        weight = factor * weight
    slot = lax.broadcasted_iota(jnp.int32, (capacity, toks), 0).astype(F32)
    for e in range(half):
        at = rank[e : e + 1, :] == slot
        rows = slice(e * capacity, (e + 1) * capacity)
        pick_ref[rows, :] = jnp.where(at, 1.0, 0.0)
        if weighted_ref is not None:
            weighted_ref[rows, :] = jnp.where(at, weight[e : e + 1, :], 0.0)


def gather_kernel(top, half, capacity, first_ref, info_ref, x_ref, out_ref, pick_ref):
    slot_tables(top, half, capacity, first_ref[0], info_ref[...], pick_ref)
    out_ref[...] = dot(pick_ref[...].astype(BF16), x_ref[...], ((1,), (0,))).astype(BF16)


def cot_kernel(top, half, capacity, first_ref, info_ref, info2_ref, x_ref, x2_ref, out_ref, pick_ref, weight_ref):
    width = x_ref.shape[1]
    lane = lax.broadcasted_iota(jnp.int32, (out_ref.shape[0], LANES), 1)
    facts = jnp.zeros((out_ref.shape[0], LANES), F32)
    for i, (info_in, x) in enumerate(((info_ref, x_ref), (info2_ref, x2_ref))):
        info = info_in[...]
        slot_tables(top, half, capacity, first_ref[0], info, pick_ref, weight_ref)
        pick = pick_ref[...]
        rows = dot(pick.astype(BF16), x[...], ((1,), (0,)))
        out_ref[:, i * width : (i + 1) * width] = rows.astype(BF16)
        share = jnp.sum(weight_ref[...], axis=1, keepdims=True)
        high = share.astype(BF16).astype(F32)
        middle = (share - high).astype(BF16).astype(F32)
        flags = info[2 * top : 2 * top + 2, :]
        marks = [jnp.sum(pick * flags[k : k + 1, :], axis=1, keepdims=True) for k in range(2)]
        counts = jnp.sum(flags, axis=1, keepdims=True)
        columns = [high, middle, share - high - middle, marks[0], marks[1], counts[0:1, :], counts[1:2, :]]
        for k, column in enumerate(columns):
            facts = jnp.where(lane == i * LANES // 2 + k, column, facts)
    out_ref[:, 2 * width :] = facts.astype(BF16)


def spread_kernel(top, half, capacity, first_ref, info_ref, info2_ref, *refs):
    outs, (pick_ref, weight_ref) = refs[:-2], refs[-2:]
    for i, info in enumerate((info_ref, info2_ref)):
        slot_tables(top, half, capacity, first_ref[0], info[...], pick_ref, weight_ref)
        weight = weight_ref[...]
        high = weight.astype(BF16)
        outs[2 * i][...] = high
        outs[2 * i + 1][...] = (weight - high.astype(F32)).astype(BF16)


def mix_kernel(high_ref, low_ref, back_ref, *rest):
    far_refs, out_ref = rest[:-1], rest[-1]
    back = back_ref[...]
    total = dot(high_ref[...], back, ((0,), (0,))) + dot(low_ref[...], back, ((0,), (0,)))
    for far in far_refs:
        total = total + far[...].astype(F32)
    out_ref[...] = total.astype(BF16)


def halve_kernel(core_ref, x_ref, out_ref, sem):
    width = out_ref.shape[1]
    mine = pl.ds(pl.multiple_of(core_ref[0] * width, LANES), width)
    copy = pltpu.make_async_copy(x_ref.at[:, mine], out_ref, sem)
    copy.start()
    copy.wait()


def add_kernel(a_ref, b_ref, out_ref):
    out_ref[...] = (a_ref[...].astype(F32) + b_ref[...].astype(F32)).astype(BF16)


def spans_of(at_ref, first, count, width):
    return [pl.ds(pl.multiple_of(at_ref[first + i], LANES), width) for i in range(count)]


def copier(sems):
    started = []

    def copy(src, dst):
        started.append(pltpu.make_async_copy(src, dst, sems.at[len(started)]))
        started[-1].start()
        return started[-1]

    return copy


def block(ref, j, step):
    return ref.at[pl.ds(j * step, step)]


def stacked(copy, srcs, dst, begin=0):
    slots, width = dst.shape[0] // 2, dst.shape[1]
    if len(srcs) == 1:
        views = [srcs[0].at[:, pl.ds(i * width, width)] for i in range(2)]
    else:
        views = [src.at[:, pl.ds(begin, width)] for src in srcs]
    return [copy(view, block(dst, i, slots)) for i, view in enumerate(views)]


def forward_kernel(pieces, out_pieces, step, at_ref, *refs):
    n = pieces
    xs_in, weights_in, refs = refs[: 2 * n], refs[2 * n : 2 * n + 3], refs[2 * n + 3 :]
    outs, refs = refs[: 3 + 2 * out_pieces], refs[3 + 2 * out_pieces :]
    xs, (gate_w, up_w, down_w), refs = refs[:n], refs[n : n + 3], refs[n + 3 :]
    (keep_gate, keep_up, hidden_ref), own, sems = refs[:3], refs[3:-1], refs[-1]
    copy = copier(sems)
    slots, width = own[0].shape
    spans = spans_of(at_ref, 0, n, xs[0].shape[1])
    out_spans = spans_of(at_ref, n, out_pieces, width)
    blocks = gate_w.shape[0] // step
    x_copies = [started for i, dst in enumerate(xs) for started in stacked(copy, xs_in[i::n], dst)]
    gate_copies, up_copies = [], []
    for j in range(blocks):
        gate_copies.append(copy(block(weights_in[0], j, step), block(gate_w, j, step)))
        up_copies.append(copy(block(weights_in[1], j, step), block(up_w, j, step)))
    down_copy = copy(weights_in[2], down_w)
    for started in x_copies:
        started.wait()
    for j in range(blocks):
        gate_copies[j].wait()
        up_copies[j].wait()
        units = slice(j * step, (j + 1) * step)
        gate = sum(dot(x[...], gate_w[units, span], ((1,), (1,))) for x, span in zip(xs, spans))
        up = sum(dot(x[...], up_w[units, span], ((1,), (1,))) for x, span in zip(xs, spans))
        s = jax.nn.sigmoid(gate)
        silu = gate * s
        keep_gate[:, units] = (up * s * (1.0 + gate * (1.0 - s))).astype(BF16)
        keep_up[:, units] = silu.astype(BF16)
        hidden_ref[:, units] = (silu * up).astype(BF16)
    out_copies = [copy(src, dst) for src, dst in zip((keep_gate, keep_up, hidden_ref), outs[:3])]
    down_copy.wait()
    for i in reversed(range(out_pieces)):
        both = dot(hidden_ref[...], down_w[:, out_spans[i]], ((1,), (0,))).astype(BF16)
        own[i][...] = both[:slots]
        out_copies.append(copy(own[i], outs[3 + out_pieces + i]))
        outs[3 + i][...] = both[slots:]
    for started in out_copies:
        started.wait()


def gradients_kernel(pieces, cot_pieces, capacity, scale, step, at_ref, *refs):
    n, m = pieces, cot_pieces
    cots_in, toks_in, refs = refs[:m], refs[m : m + 2 * n], refs[m + 2 * n :]
    facts_in, inputs, refs = refs[0], refs[1:5], refs[5:]
    outs, cots, toks, refs = refs[:3], refs[3 : 3 + m], refs[3 + m : 3 + m + n], refs[3 + m + n :]
    down_w, keep_gate, keep_up, hidden, dgate, dup, facts_ref, turned, held, sems = refs
    copy = copier(sems)
    spans = spans_of(at_ref, 0, n, toks[0].shape[1])
    spans = spans_of(at_ref, n, m, cots[0].shape[1])
    facts_copy = copy(facts_in.at[:, pl.ds(facts_in.shape[1] - LANES, LANES)], facts_ref)
    hidden_copy = copy(inputs[3], hidden)
    cot_copies = [stacked(copy, [src], dst) for src, dst in zip(cots_in, cots)]
    down_copy = copy(inputs[0], down_w)
    keep_copies = [copy(inputs[1], keep_gate), copy(inputs[2], keep_up)]
    tok_copies = [stacked(copy, toks_in[i::n], dst) for i, dst in enumerate(toks)]
    facts_copy.wait()
    facts = facts_ref[...].astype(F32)
    slots, side = facts.shape[0], LANES // 2
    total = jnp.zeros((1, LANES), F32)
    for row in range(0, slots, capacity):
        total = total + facts[row : row + 1, :]
    retain_all = total[:, 5:6] + total[:, side + 5 : side + 6]
    forget_all = total[:, 6:7] + total[:, side + 6 : side + 7]

    def weight_of(begin):
        share, retain, forget = facts[:, begin : begin + 3], facts[:, begin + 3 : begin + 4], facts[:, begin + 4 : begin + 5]
        coefficient = scale * (retain / retain_all - forget / forget_all)
        return coefficient * (share[:, 0:1] + share[:, 1:2] + share[:, 2:3])

    slot_weights = [weight_of(0), weight_of(side)]
    for i in range(m):
        for started in cot_copies[i]:
            started.wait()
        for part in range(2):
            rows = slice(part * slots, (part + 1) * slots)
            cots[i][rows, :] = (slot_weights[part] * cots[i][rows, :].astype(F32)).astype(BF16)
    done = [[] for _ in range(max(n, m))]
    written = []

    def outer(left, xs, spans, copies, k):
        turned[...] = left[...].T
        for i, (x, span) in enumerate(zip(xs, spans)):
            for started in copies[i]:
                started.wait()
            width = x.shape[1]
            place = slice(i * width, (i + 1) * width)
            held[k, :, place] = dot(turned[...], x[...], ((1,), (0,))).astype(BF16)
            written.append(copy(held.at[k, :, pl.ds(i * width, width)], outs[k].at[:, span]))

    hidden_copy.wait()
    outer(hidden, cots, spans, done, 2)
    down_copy.wait()
    for started in keep_copies:
        started.wait()
    for begin in range(0, down_w.shape[0], step):
        units = slice(begin, begin + step)
        dhidden = sum(dot(x[...], down_w[units, span], ((1,), (1,))) for x, span in zip(cots, spans))
        dgate[:, units] = (dhidden * keep_gate[:, units].astype(F32)).astype(BF16)
        dup[:, units] = (dhidden * keep_up[:, units].astype(F32)).astype(BF16)
    outer(dgate, toks, spans, tok_copies, 0)
    outer(dup, toks, spans, done, 1)
    for started in written:
        started.wait()


def body(
    tokens,
    cotangent,
    expert_ids,
    route_weight,
    forget_mask,
    lengths,
    gate_weight,
    up_weight,
    down_weight,
):
    tok_rows, features = tokens.shape
    top = expert_ids.shape[1]
    owners = lax.axis_size("dp")
    parts = lax.axis_size("tensor")
    half = owners // 2
    width = features // parts
    capacity = 5 * tok_rows * top // (4 * owners)
    slots = half * capacity
    seq_len = tok_rows * owners // lengths.shape[0]
    me = lax.axis_index("dp")
    core = lax.axis_index("tensor")
    mates = [(i, (i + half) % owners) for i in range(owners)]
    halves = [list(range(half)), list(range(half, owners))]
    first = ((me // half) * half).astype(jnp.int32).reshape(1)
    place = (me * tok_rows).astype(jnp.int32).reshape(1)
    shape = jax.ShapeDtypeStruct
    table = pltpu.VMEM((slots, tok_rows), F32)
    limit = pltpu.CompilerParams(vmem_limit_bytes=8 * 2**20)

    def to_mate(value):
        return lax.ppermute(value, "dp", mates)

    def exchange(value):
        value = value.reshape(half, value.shape[0] // half, value.shape[1])
        return lax.all_to_all(
            value, "dp", split_axis=0, concat_axis=0, axis_index_groups=halves, tiled=True
        )

    def swapped(value):
        return lax.ppermute(value, "tensor", [(0, 1), (1, 0)])

    def my_features(value, micros):
        return pl.pallas_call(
            halve_kernel,
            out_shape=shape((tok_rows, width), BF16),
            in_specs=[SMEM, HBM],
            out_specs=VMEM,
            scratch_shapes=[pltpu.SemaphoreType.DMA],
            compiler_params=limit,
            cost_estimate=cost(micros),
        )(core.astype(jnp.int32).reshape(1), in_hbm(value))

    def after(value, *others):
        return lax.optimization_barrier((value, *others))[0]

    def mixed_rows(spread, back, *far):
        return pl.pallas_call(
            mix_kernel,
            out_shape=shape((tok_rows, width), BF16),
            in_specs=[VMEM] * (3 + len(far)),
            out_specs=VMEM,
            compiler_params=limit,
            cost_estimate=cost(1),
        )(*spread, back, *far)

    tok_mine = my_features(tokens, 1)
    tok_mate = to_mate(tok_mine)
    expert_ids = after(expert_ids, tok_mine)
    about = pl.pallas_call(
        functools.partial(facts_kernel, top, seq_len),
        out_shape=jax.ShapeDtypeStruct((FACTS, tok_rows), F32),
        in_specs=[SMEM, SMEM, VMEM, VMEM, VMEM],
        out_specs=VMEM,
        compiler_params=limit,
        cost_estimate=cost(1),
    )(place, lengths, expert_ids.T, route_weight.T, forget_mask.reshape(1, tok_rows))
    about_mate = to_mate(about)

    def gathered(info, x, micros):
        return pl.pallas_call(
            functools.partial(gather_kernel, top, half, capacity),
            out_shape=shape((slots, width), BF16),
            in_specs=[SMEM, VMEM, VMEM],
            out_specs=VMEM,
            scratch_shapes=[table],
            compiler_params=limit,
            cost_estimate=cost(micros),
        )(first, info, x)

    recv_own = exchange(gathered(about, tok_mine, 1)).reshape(slots, width)
    send_mate = gathered(about_mate, tok_mate, 20)
    recv_mate = exchange(after(send_mate, recv_own)).reshape(slots, width)

    spreads = pl.pallas_call(
        functools.partial(spread_kernel, top, half, capacity),
        out_shape=[shape((slots, tok_rows), BF16)] * 4,
        in_specs=[SMEM, VMEM, VMEM],
        out_specs=[VMEM] * 4,
        scratch_shapes=[table, table],
        compiler_params=limit,
        cost_estimate=cost(1),
    )(first, about, about_mate)

    cot_mine = my_features(after(cotangent, about), 1)
    cot_mate = to_mate(after(cot_mine, tok_mate))
    send_cot = pl.pallas_call(
        functools.partial(cot_kernel, top, half, capacity),
        out_shape=shape((slots, 2 * width + LANES), BF16),
        in_specs=[SMEM] + [VMEM] * 4,
        out_specs=VMEM,
        scratch_shapes=[table, table],
        compiler_params=limit,
        cost_estimate=cost(15),
    )(first, about, about_mate, cot_mine, cot_mate)
    recv_own, recv_mate = after(recv_own, send_cot), after(recv_mate, send_cot)
    recv_cot = exchange(after(send_cot, recv_mate)).reshape(slots, 2 * width + LANES)

    gate_w, up_w, down_w = gate_weight[0], up_weight[0], down_weight[0]
    weights = [in_hbm(w) for w in (gate_w, up_w, down_w)]
    units = gate_w.shape[0]
    step = min(units, 256)
    blocks = units // step

    def all_features(row):
        return lax.all_gather(row, "tensor", axis=1, tiled=True)

    if parts == 2:
        other_own = swapped(recv_own)
        toks = [recv_own, other_own, recv_mate, swapped(after(recv_mate, other_own))]
        starts = [core * width, (1 - core) * width] * 2
        span = width
    else:
        toks = [all_features(recv_own), all_features(recv_mate)]
        starts = [core * 0] * 2
        span = features
    at = jnp.stack(starts).astype(jnp.int32)
    toks = [in_hbm(x) for x in toks]
    n = m = len(toks) // 2
    weight_buffer = pltpu.VMEM((units, features), BF16)
    unit_rows = ((2 * slots, units), BF16)
    tok_buffers = [pltpu.VMEM((2 * slots, span), BF16)] * n
    cot_buffers = [pltpu.VMEM((2 * slots, span), BF16)] * m
    roomy = pltpu.CompilerParams(vmem_limit_bytes=36 * 2**20)

    def summed(outs):
        if parts != 2:
            return lax.psum_scatter(outs[0], "tensor", scatter_dimension=1, tiled=True)
        return pl.pallas_call(
            add_kernel,
            out_shape=shape((slots, width), BF16),
            in_specs=[VMEM] * 2,
            out_specs=VMEM,
            compiler_params=limit,
            cost_estimate=cost(1),
        )(outs[0], swapped(outs[1]))

    piece = (slots, span)
    keep_gate, keep_up, hidden, *outs = pl.pallas_call(
        functools.partial(forward_kernel, n, m, step),
        out_shape=[pltpu.HBM(*unit_rows)] * 3
        + [shape(piece, BF16)] * m
        + [pltpu.HBM(piece, BF16)] * m,
        in_specs=[SMEM] + [HBM] * (2 * n + 3),
        out_specs=[HBM] * 3 + [VMEM] * m + [HBM] * m,
        scratch_shapes=tok_buffers
        + [weight_buffer] * 3
        + [pltpu.VMEM(*unit_rows)] * 3
        + [pltpu.VMEM(piece, BF16)] * m
        + [pltpu.SemaphoreType.DMA((2 * n + 2 * blocks + 4 + m,))],
        compiler_params=roomy,
        cost_estimate=cost(8),
    )(at, *toks, *weights)
    out_mate = summed(outs[:m])
    back_mate = exchange(out_mate).reshape(slots, width)
    out_own = summed(outs[m:])

    recv_cot = after(recv_cot, out_mate)
    if parts == 2:
        cots = [recv_cot, swapped(recv_cot)]
    else:
        both = [all_features(recv_cot[:, i * width : (i + 1) * width]) for i in range(2)]
        cots = [jnp.concatenate(both, axis=1)]
    mix_mate = mixed_rows(spreads[2:], back_mate)
    mix_far = to_mate(mix_mate)
    keeps = [in_hbm(x) for x in (keep_gate, keep_up, after(hidden, mix_mate))]
    grad_gate, grad_up, grad_down = pl.pallas_call(
        functools.partial(gradients_kernel, n, m, capacity, float(top * tok_rows), step),
        out_shape=[pltpu.HBM((units, features), BF16)] * 3,
        in_specs=[SMEM] + [HBM] * (2 * n + m + 5),
        out_specs=[HBM] * 3,
        scratch_shapes=cot_buffers
        + tok_buffers
        + [weight_buffer]
        + [pltpu.VMEM(*unit_rows)] * 5
        + [
            pltpu.VMEM((slots, LANES), BF16),
            pltpu.VMEM((units, 2 * slots), BF16),
            pltpu.VMEM((3, units, features), BF16),
            pltpu.SemaphoreType.DMA((4 * n + 3 * m + 5,)),
        ],
        compiler_params=roomy,
        cost_estimate=cost(20),
    )(at, *[in_hbm(x) for x in cots], *toks, in_hbm(recv_cot), weights[2], *keeps)
    back_own = exchange(after(out_own, mix_mate)).reshape(slots, width)
    mixed = mixed_rows([after(spreads[0], grad_down), spreads[1]], back_own, mix_far)
    return (
        mixed,
        grad_gate[None],
        grad_up[None],
        grad_down[None],
    )


def solution(mesh):
    in_specs = (
        P("dp", None),
        P("dp", None),
        P("dp", None),
        P("dp", None),
        P("dp"),
        P(),
        P("dp", "tensor", None),
        P("dp", "tensor", None),
        P("dp", "tensor", None),
    )
    out_specs = (
        P("dp", "tensor"),
        P("dp", "tensor", None),
        P("dp", "tensor", None),
        P("dp", "tensor", None),
    )
    return jax.shard_map(body, mesh=mesh, in_specs=in_specs, out_specs=out_specs, check_vma=False)
```

```python
import functools

import jax
import jax.numpy as jnp
from jax import lax
from jax.experimental import pallas as pl
from jax.experimental.pallas import tpu as pltpu
from jax.sharding import PartitionSpec as P

F32 = jnp.float32
BF16 = jnp.bfloat16
LANES = 128
FACTS = 16
VMEM = pl.BlockSpec(memory_space=pltpu.VMEM)
SMEM = pl.BlockSpec(memory_space=pltpu.SMEM)
ANY = pl.BlockSpec(memory_space=pl.ANY)
HBM = pl.BlockSpec(memory_space=pltpu.HBM)


def cost(micros):
    return pl.CostEstimate(
        flops=int(micros * 1e9), bytes_accessed=int(micros * 3e6), transcendentals=0
    )


def in_hbm(value):
    return pltpu.with_memory_space_constraint(value, pltpu.HBM)


def dot(a, b, dims):
    return lax.dot_general(a, b, (dims, ((), ())), preferred_element_type=F32)


def facts_kernel(top, seq_len, place_ref, lengths_ref, ids_ref, weight_ref, forget_ref, out_ref):
    toks = ids_ref.shape[1]
    weight = weight_ref[...]
    out_ref[:top, :] = ids_ref[...].astype(F32)
    out_ref[top : 2 * top, :] = weight / jnp.sum(weight, axis=0, keepdims=True)
    token = place_ref[0] + lax.broadcasted_iota(jnp.int32, (1, toks), 1)
    valid = jnp.zeros((1, toks), jnp.int32)
    for s in range(lengths_ref.shape[0]):
        begin = s * seq_len
        inside = (token >= begin) & (token < begin + lengths_ref[s])
        valid = jnp.where(inside, 1, valid)
    forget = valid * forget_ref[...]
    out_ref[2 * top : 2 * top + 1, :] = (valid - forget).astype(F32)
    out_ref[2 * top + 1 : 2 * top + 2, :] = forget.astype(F32)
    rest = 2 * top + 2
    out_ref[rest:, :] = jnp.zeros((out_ref.shape[0] - rest, toks), F32)


def slot_tables(top, half, capacity, first, info, pick_ref, weighted_ref=None, factor=None):
    toks = info.shape[1]
    expert = (first + lax.broadcasted_iota(jnp.int32, (half, toks), 0)).astype(F32)
    named = jnp.zeros((half, toks), F32)
    weight = jnp.zeros((half, toks), F32)
    for k in range(top):
        hit = info[k : k + 1, :] == expert
        named = jnp.where(hit, 1.0, named)
        weight = jnp.where(hit, info[top + k : top + k + 1, :], weight)
    row = lax.broadcasted_iota(jnp.int32, (toks, toks), 0)
    column = lax.broadcasted_iota(jnp.int32, (toks, toks), 1)
    earlier = jnp.where(row < column, 1.0, 0.0).astype(BF16)
    rank = dot(named.astype(BF16), earlier, ((1,), (0,)))
    rank = jnp.where(named > 0.0, rank, -1.0)
    if factor is not None:
        weight = factor * weight
    slot = lax.broadcasted_iota(jnp.int32, (capacity, toks), 0).astype(F32)
    for e in range(half):
        at = rank[e : e + 1, :] == slot
        rows = slice(e * capacity, (e + 1) * capacity)
        pick_ref[rows, :] = jnp.where(at, 1.0, 0.0)
        if weighted_ref is not None:
            weighted_ref[rows, :] = jnp.where(at, weight[e : e + 1, :], 0.0)


def gather_kernel(top, half, capacity, first_ref, info_ref, x_ref, out_ref, pick_ref):
    slot_tables(top, half, capacity, first_ref[0], info_ref[...], pick_ref)
    out_ref[...] = dot(pick_ref[...].astype(BF16), x_ref[...], ((1,), (0,))).astype(BF16)


def cot_kernel(top, half, capacity, first_ref, info_ref, info2_ref, x_ref, x2_ref, out_ref, pick_ref, weight_ref):
    width = x_ref.shape[1]
    lane = lax.broadcasted_iota(jnp.int32, (out_ref.shape[0], LANES), 1)
    facts = jnp.zeros((out_ref.shape[0], LANES), F32)
    for i, (info_in, x) in enumerate(((info_ref, x_ref), (info2_ref, x2_ref))):
        info = info_in[...]
        slot_tables(top, half, capacity, first_ref[0], info, pick_ref, weight_ref)
        pick = pick_ref[...]
        rows = dot(pick.astype(BF16), x[...], ((1,), (0,)))
        out_ref[:, i * width : (i + 1) * width] = rows.astype(BF16)
        share = jnp.sum(weight_ref[...], axis=1, keepdims=True)
        high = share.astype(BF16).astype(F32)
        middle = (share - high).astype(BF16).astype(F32)
        flags = info[2 * top : 2 * top + 2, :]
        marks = [jnp.sum(pick * flags[k : k + 1, :], axis=1, keepdims=True) for k in range(2)]
        counts = jnp.sum(flags, axis=1, keepdims=True)
        columns = [high, middle, share - high - middle, marks[0], marks[1], counts[0:1, :], counts[1:2, :]]
        for k, column in enumerate(columns):
            facts = jnp.where(lane == i * LANES // 2 + k, column, facts)
    out_ref[:, 2 * width :] = facts.astype(BF16)


def spread_kernel(top, half, capacity, first_ref, info_ref, info2_ref, *refs):
    outs, (pick_ref, weight_ref) = refs[:-2], refs[-2:]
    for i, info in enumerate((info_ref, info2_ref)):
        slot_tables(top, half, capacity, first_ref[0], info[...], pick_ref, weight_ref)
        weight = weight_ref[...]
        high = weight.astype(BF16)
        outs[2 * i][...] = high
        outs[2 * i + 1][...] = (weight - high.astype(F32)).astype(BF16)


def mix_kernel(high_ref, low_ref, back_ref, *rest):
    far_refs, out_ref = rest[:-1], rest[-1]
    back = back_ref[...]
    total = dot(high_ref[...], back, ((0,), (0,))) + dot(low_ref[...], back, ((0,), (0,)))
    for far in far_refs:
        total = total + far[...].astype(F32)
    out_ref[...] = total.astype(BF16)


def halve_kernel(core_ref, x_ref, out_ref, sem):
    width = out_ref.shape[1]
    mine = pl.ds(pl.multiple_of(core_ref[0] * width, LANES), width)
    copy = pltpu.make_async_copy(x_ref.at[:, mine], out_ref, sem)
    copy.start()
    copy.wait()


def add_kernel(a_ref, b_ref, out_ref):
    out_ref[...] = (a_ref[...].astype(F32) + b_ref[...].astype(F32)).astype(BF16)


def spans_of(at_ref, first, count, width):
    return [pl.ds(pl.multiple_of(at_ref[first + i], LANES), width) for i in range(count)]


def copier(sems):
    started = []

    def copy(src, dst):
        started.append(pltpu.make_async_copy(src, dst, sems.at[len(started)]))
        started[-1].start()
        return started[-1]

    return copy


def block(ref, j, step):
    return ref.at[pl.ds(j * step, step)]


def stacked(copy, srcs, dst, begin=0):
    slots, width = dst.shape[0] // 2, dst.shape[1]
    if len(srcs) == 1:
        views = [srcs[0].at[:, pl.ds(i * width, width)] for i in range(2)]
    else:
        views = [src.at[:, pl.ds(begin, width)] for src in srcs]
    return [copy(view, block(dst, i, slots)) for i, view in enumerate(views)]


def forward_kernel(pieces, out_pieces, step, at_ref, *refs):
    n = pieces
    xs_in, weights_in, refs = refs[: 2 * n], refs[2 * n : 2 * n + 3], refs[2 * n + 3 :]
    outs, refs = refs[: 3 + 2 * out_pieces], refs[3 + 2 * out_pieces :]
    xs, (gate_w, up_w, down_w), refs = refs[:n], refs[n : n + 3], refs[n + 3 :]
    (keep_gate, keep_up, hidden_ref), own, sems = refs[:3], refs[3:-1], refs[-1]
    copy = copier(sems)
    slots, width = own[0].shape
    spans = spans_of(at_ref, 0, n, xs[0].shape[1])
    out_spans = spans_of(at_ref, n, out_pieces, width)
    blocks = gate_w.shape[0] // step
    x_copies = [started for i, dst in enumerate(xs) for started in stacked(copy, xs_in[i::n], dst)]
    gate_copies, up_copies = [], []
    for j in range(blocks):
        gate_copies.append(copy(block(weights_in[0], j, step), block(gate_w, j, step)))
        up_copies.append(copy(block(weights_in[1], j, step), block(up_w, j, step)))
    down_copy = copy(weights_in[2], down_w)
    for started in x_copies:
        started.wait()
    for j in range(blocks):
        gate_copies[j].wait()
        up_copies[j].wait()
        units = slice(j * step, (j + 1) * step)
        gate = sum(dot(x[...], gate_w[units, span], ((1,), (1,))) for x, span in zip(xs, spans))
        up = sum(dot(x[...], up_w[units, span], ((1,), (1,))) for x, span in zip(xs, spans))
        s = jax.nn.sigmoid(gate)
        silu = gate * s
        keep_gate[:, units] = (up * s * (1.0 + gate * (1.0 - s))).astype(BF16)
        keep_up[:, units] = silu.astype(BF16)
        hidden_ref[:, units] = (silu * up).astype(BF16)
    out_copies = [copy(src, dst) for src, dst in zip((keep_gate, keep_up, hidden_ref), outs[:3])]
    down_copy.wait()
    for i in reversed(range(out_pieces)):
        both = dot(hidden_ref[...], down_w[:, out_spans[i]], ((1,), (0,))).astype(BF16)
        own[i][...] = both[:slots]
        out_copies.append(copy(own[i], outs[3 + out_pieces + i]))
        outs[3 + i][...] = both[slots:]
    for started in out_copies:
        started.wait()


def gradients_kernel(pieces, cot_pieces, capacity, scale, step, at_ref, *refs):
    n, m = pieces, cot_pieces
    cots_in, toks_in, refs = refs[:m], refs[m : m + 2 * n], refs[m + 2 * n :]
    facts_in, inputs, refs = refs[0], refs[1:5], refs[5:]
    outs, cots, toks, refs = refs[:3], refs[3 : 3 + m], refs[3 + m : 3 + m + n], refs[3 + m + n :]
    down_w, keep_gate, keep_up, hidden, dgate, dup, facts_ref, turned, held, sems = refs
    copy = copier(sems)
    spans = spans_of(at_ref, 0, n, toks[0].shape[1])
    spans = spans_of(at_ref, n, m, cots[0].shape[1])
    facts_copy = copy(facts_in.at[:, pl.ds(facts_in.shape[1] - LANES, LANES)], facts_ref)
    hidden_copy = copy(inputs[3], hidden)
    cot_copies = [stacked(copy, [src], dst) for src, dst in zip(cots_in, cots)]
    down_copy = copy(inputs[0], down_w)
    keep_copies = [copy(inputs[1], keep_gate), copy(inputs[2], keep_up)]
    tok_copies = [stacked(copy, toks_in[i::n], dst) for i, dst in enumerate(toks)]
    facts_copy.wait()
    facts = facts_ref[...].astype(F32)
    slots, side = facts.shape[0], LANES // 2
    total = jnp.zeros((1, LANES), F32)
    for row in range(0, slots, capacity):
        total = total + facts[row : row + 1, :]
    retain_all = total[:, 5:6] + total[:, side + 5 : side + 6]
    forget_all = total[:, 6:7] + total[:, side + 6 : side + 7]

    def weight_of(begin):
        share, retain, forget = facts[:, begin : begin + 3], facts[:, begin + 3 : begin + 4], facts[:, begin + 4 : begin + 5]
        coefficient = scale * (retain / retain_all - forget / forget_all)
        return coefficient * (share[:, 0:1] + share[:, 1:2] + share[:, 2:3])

    slot_weights = [weight_of(0), weight_of(side)]
    for i in range(m):
        for started in cot_copies[i]:
            started.wait()
        for part in range(2):
            rows = slice(part * slots, (part + 1) * slots)
            cots[i][rows, :] = (slot_weights[part] * cots[i][rows, :].astype(F32)).astype(BF16)
    done = [[] for _ in range(max(n, m))]
    written = []

    def outer(left, xs, spans, copies, k):
        turned[...] = left[...].T
        for i, (x, span) in enumerate(zip(xs, spans)):
            for started in copies[i]:
                started.wait()
            width = x.shape[1]
            place = slice(i * width, (i + 1) * width)
            held[k, :, place] = dot(turned[...], x[...], ((1,), (0,))).astype(BF16)
            written.append(copy(held.at[k, :, pl.ds(i * width, width)], outs[k].at[:, span]))

    hidden_copy.wait()
    outer(hidden, cots, spans, done, 2)
    down_copy.wait()
    for started in keep_copies:
        started.wait()
    for begin in range(0, down_w.shape[0], step):
        units = slice(begin, begin + step)
        dhidden = sum(dot(x[...], down_w[units, span], ((1,), (1,))) for x, span in zip(cots, spans))
        dgate[:, units] = (dhidden * keep_gate[:, units].astype(F32)).astype(BF16)
        dup[:, units] = (dhidden * keep_up[:, units].astype(F32)).astype(BF16)
    outer(dgate, toks, spans, tok_copies, 0)
    outer(dup, toks, spans, done, 1)
    for started in written:
        started.wait()


def body(
    tokens,
    cotangent,
    expert_ids,
    route_weight,
    forget_mask,
    lengths,
    gate_weight,
    up_weight,
    down_weight,
):
    tok_rows, features = tokens.shape
    top = expert_ids.shape[1]
    owners = lax.axis_size("dp")
    parts = lax.axis_size("tensor")
    half = owners // 2
    width = features // parts
    capacity = 5 * tok_rows * top // (4 * owners)
    slots = half * capacity
    seq_len = tok_rows * owners // lengths.shape[0]
    me = lax.axis_index("dp")
    core = lax.axis_index("tensor")
    mates = [(i, (i + half) % owners) for i in range(owners)]
    halves = [list(range(half)), list(range(half, owners))]
    first = ((me // half) * half).astype(jnp.int32).reshape(1)
    place = (me * tok_rows).astype(jnp.int32).reshape(1)
    shape = jax.ShapeDtypeStruct
    table = pltpu.VMEM((slots, tok_rows), F32)
    limit = pltpu.CompilerParams(vmem_limit_bytes=8 * 2**20)

    def to_mate(value):
        return lax.ppermute(value, "dp", mates)

    def exchange(value):
        value = value.reshape(half, value.shape[0] // half, value.shape[1])
        return lax.all_to_all(
            value, "dp", split_axis=0, concat_axis=0, axis_index_groups=halves, tiled=True
        )

    def swapped(value):
        return lax.ppermute(value, "tensor", [(0, 1), (1, 0)])

    def my_features(value, micros):
        return pl.pallas_call(
            halve_kernel,
            out_shape=shape((tok_rows, width), BF16),
            in_specs=[SMEM, HBM],
            out_specs=VMEM,
            scratch_shapes=[pltpu.SemaphoreType.DMA],
            compiler_params=limit,
            cost_estimate=cost(micros),
        )(core.astype(jnp.int32).reshape(1), in_hbm(value))

    def after(value, *others):
        return lax.optimization_barrier((value, *others))[0]

    def mixed_rows(spread, back, *far):
        return pl.pallas_call(
            mix_kernel,
            out_shape=shape((tok_rows, width), BF16),
            in_specs=[VMEM] * (3 + len(far)),
            out_specs=VMEM,
            compiler_params=limit,
            cost_estimate=cost(1),
        )(*spread, back, *far)

    tok_mine = my_features(tokens, 1)
    tok_mate = to_mate(tok_mine)
    expert_ids = after(expert_ids, tok_mine)
    about = pl.pallas_call(
        functools.partial(facts_kernel, top, seq_len),
        out_shape=jax.ShapeDtypeStruct((FACTS, tok_rows), F32),
        in_specs=[SMEM, SMEM, VMEM, VMEM, VMEM],
        out_specs=VMEM,
        compiler_params=limit,
        cost_estimate=cost(1),
    )(place, lengths, expert_ids.T, route_weight.T, forget_mask.reshape(1, tok_rows))
    about_mate = to_mate(about)

    def gathered(info, x, micros):
        return pl.pallas_call(
            functools.partial(gather_kernel, top, half, capacity),
            out_shape=shape((slots, width), BF16),
            in_specs=[SMEM, VMEM, VMEM],
            out_specs=VMEM,
            scratch_shapes=[table],
            compiler_params=limit,
            cost_estimate=cost(micros),
        )(first, info, x)

    recv_own = exchange(gathered(about, tok_mine, 1)).reshape(slots, width)
    send_mate = gathered(about_mate, tok_mate, 20)
    recv_mate = exchange(after(send_mate, recv_own)).reshape(slots, width)

    spreads = pl.pallas_call(
        functools.partial(spread_kernel, top, half, capacity),
        out_shape=[shape((slots, tok_rows), BF16)] * 4,
        in_specs=[SMEM, VMEM, VMEM],
        out_specs=[VMEM] * 4,
        scratch_shapes=[table, table],
        compiler_params=limit,
        cost_estimate=cost(1),
    )(first, about, about_mate)

    cot_mine = my_features(after(cotangent, about), 1)
    cot_mate = to_mate(after(cot_mine, send_mate))
    send_cot = pl.pallas_call(
        functools.partial(cot_kernel, top, half, capacity),
        out_shape=shape((slots, 2 * width + LANES), BF16),
        in_specs=[SMEM] + [VMEM] * 4,
        out_specs=VMEM,
        scratch_shapes=[table, table],
        compiler_params=limit,
        cost_estimate=cost(15),
    )(first, about, about_mate, cot_mine, cot_mate)
    recv_own, recv_mate = after(recv_own, send_cot), after(recv_mate, send_cot)
    recv_cot = exchange(after(send_cot, recv_mate)).reshape(slots, 2 * width + LANES)

    gate_w, up_w, down_w = gate_weight[0], up_weight[0], down_weight[0]
    weights = [in_hbm(w) for w in (gate_w, up_w, down_w)]
    units = gate_w.shape[0]
    step = min(units, 256)
    blocks = units // step

    def all_features(row):
        return lax.all_gather(row, "tensor", axis=1, tiled=True)

    if parts == 2:
        other_own = swapped(recv_own)
        toks = [recv_own, other_own, recv_mate, swapped(after(recv_mate, other_own))]
        starts = [core * width, (1 - core) * width] * 2
        span = width
    else:
        toks = [all_features(recv_own), all_features(recv_mate)]
        starts = [core * 0] * 2
        span = features
    at = jnp.stack(starts).astype(jnp.int32)
    toks = [in_hbm(x) for x in toks]
    n = m = len(toks) // 2
    weight_buffer = pltpu.VMEM((units, features), BF16)
    unit_rows = ((2 * slots, units), BF16)
    tok_buffers = [pltpu.VMEM((2 * slots, span), BF16)] * n
    cot_buffers = [pltpu.VMEM((2 * slots, span), BF16)] * m
    roomy = pltpu.CompilerParams(vmem_limit_bytes=36 * 2**20)

    def summed(outs):
        if parts != 2:
            return lax.psum_scatter(outs[0], "tensor", scatter_dimension=1, tiled=True)
        return pl.pallas_call(
            add_kernel,
            out_shape=shape((slots, width), BF16),
            in_specs=[VMEM] * 2,
            out_specs=VMEM,
            compiler_params=limit,
            cost_estimate=cost(1),
        )(outs[0], swapped(outs[1]))

    piece = (slots, span)
    keep_gate, keep_up, hidden, *outs = pl.pallas_call(
        functools.partial(forward_kernel, n, m, step),
        out_shape=[pltpu.HBM(*unit_rows)] * 3
        + [shape(piece, BF16)] * m
        + [pltpu.HBM(piece, BF16)] * m,
        in_specs=[SMEM] + [HBM] * (2 * n + 3),
        out_specs=[HBM] * 3 + [VMEM] * m + [HBM] * m,
        scratch_shapes=tok_buffers
        + [weight_buffer] * 3
        + [pltpu.VMEM(*unit_rows)] * 3
        + [pltpu.VMEM(piece, BF16)] * m
        + [pltpu.SemaphoreType.DMA((2 * n + 2 * blocks + 4 + m,))],
        compiler_params=roomy,
        cost_estimate=cost(8),
    )(at, *toks, *weights)
    out_mate = summed(outs[:m])
    back_mate = exchange(out_mate).reshape(slots, width)
    out_own = summed(outs[m:])

    recv_cot = after(recv_cot, out_mate)
    if parts == 2:
        cots = [recv_cot, swapped(recv_cot)]
    else:
        both = [all_features(recv_cot[:, i * width : (i + 1) * width]) for i in range(2)]
        cots = [jnp.concatenate(both, axis=1)]
    mix_mate = mixed_rows(spreads[2:], back_mate)
    mix_far = to_mate(mix_mate)
    keeps = [in_hbm(x) for x in (keep_gate, keep_up, after(hidden, mix_mate))]
    grad_gate, grad_up, grad_down = pl.pallas_call(
        functools.partial(gradients_kernel, n, m, capacity, float(top * tok_rows), step),
        out_shape=[pltpu.HBM((units, features), BF16)] * 3,
        in_specs=[SMEM] + [HBM] * (2 * n + m + 5),
        out_specs=[HBM] * 3,
        scratch_shapes=cot_buffers
        + tok_buffers
        + [weight_buffer]
        + [pltpu.VMEM(*unit_rows)] * 5
        + [
            pltpu.VMEM((slots, LANES), BF16),
            pltpu.VMEM((units, 2 * slots), BF16),
            pltpu.VMEM((3, units, features), BF16),
            pltpu.SemaphoreType.DMA((4 * n + 3 * m + 5,)),
        ],
        compiler_params=roomy,
        cost_estimate=cost(20),
    )(at, *[in_hbm(x) for x in cots], *toks, in_hbm(recv_cot), weights[2], *keeps)
    back_own = exchange(after(out_own, mix_mate)).reshape(slots, width)
    mixed = mixed_rows([after(spreads[0], grad_down), spreads[1]], back_own, mix_far)
    return (
        mixed,
        grad_gate[None],
        grad_up[None],
        grad_down[None],
    )


def solution(mesh):
    in_specs = (
        P("dp", None),
        P("dp", None),
        P("dp", None),
        P("dp", None),
        P("dp"),
        P(),
        P("dp", "tensor", None),
        P("dp", "tensor", None),
        P("dp", "tensor", None),
    )
    out_specs = (
        P("dp", "tensor"),
        P("dp", "tensor", None),
        P("dp", "tensor", None),
        P("dp", "tensor", None),
    )
    return jax.shard_map(body, mesh=mesh, in_specs=in_specs, out_specs=out_specs, check_vma=False)
```

```python
import functools

import jax
import jax.numpy as jnp
from jax import lax
from jax.experimental import pallas as pl
from jax.experimental.pallas import tpu as pltpu
from jax.sharding import PartitionSpec as P

F32 = jnp.float32
BF16 = jnp.bfloat16
LANES = 128
FACTS = 16
VMEM = pl.BlockSpec(memory_space=pltpu.VMEM)
SMEM = pl.BlockSpec(memory_space=pltpu.SMEM)
ANY = pl.BlockSpec(memory_space=pl.ANY)
HBM = pl.BlockSpec(memory_space=pltpu.HBM)


def cost(micros):
    return pl.CostEstimate(
        flops=int(micros * 1e9), bytes_accessed=int(micros * 3e6), transcendentals=0
    )


def in_hbm(value):
    return pltpu.with_memory_space_constraint(value, pltpu.HBM)


def dot(a, b, dims):
    return lax.dot_general(a, b, (dims, ((), ())), preferred_element_type=F32)


def facts_kernel(top, seq_len, place_ref, lengths_ref, ids_ref, weight_ref, forget_ref, out_ref):
    toks = ids_ref.shape[1]
    weight = weight_ref[...]
    out_ref[:top, :] = ids_ref[...].astype(F32)
    out_ref[top : 2 * top, :] = weight / jnp.sum(weight, axis=0, keepdims=True)
    token = place_ref[0] + lax.broadcasted_iota(jnp.int32, (1, toks), 1)
    valid = jnp.zeros((1, toks), jnp.int32)
    for s in range(lengths_ref.shape[0]):
        begin = s * seq_len
        inside = (token >= begin) & (token < begin + lengths_ref[s])
        valid = jnp.where(inside, 1, valid)
    forget = valid * forget_ref[...]
    out_ref[2 * top : 2 * top + 1, :] = (valid - forget).astype(F32)
    out_ref[2 * top + 1 : 2 * top + 2, :] = forget.astype(F32)
    rest = 2 * top + 2
    out_ref[rest:, :] = jnp.zeros((out_ref.shape[0] - rest, toks), F32)


def slot_tables(top, half, capacity, first, info, pick_ref, weighted_ref=None, factor=None):
    toks = info.shape[1]
    expert = (first + lax.broadcasted_iota(jnp.int32, (half, toks), 0)).astype(F32)
    named = jnp.zeros((half, toks), F32)
    weight = jnp.zeros((half, toks), F32)
    for k in range(top):
        hit = info[k : k + 1, :] == expert
        named = jnp.where(hit, 1.0, named)
        weight = jnp.where(hit, info[top + k : top + k + 1, :], weight)
    row = lax.broadcasted_iota(jnp.int32, (toks, toks), 0)
    column = lax.broadcasted_iota(jnp.int32, (toks, toks), 1)
    earlier = jnp.where(row < column, 1.0, 0.0).astype(BF16)
    rank = dot(named.astype(BF16), earlier, ((1,), (0,)))
    rank = jnp.where(named > 0.0, rank, -1.0)
    if factor is not None:
        weight = factor * weight
    slot = lax.broadcasted_iota(jnp.int32, (capacity, toks), 0).astype(F32)
    for e in range(half):
        at = rank[e : e + 1, :] == slot
        rows = slice(e * capacity, (e + 1) * capacity)
        pick_ref[rows, :] = jnp.where(at, 1.0, 0.0)
        if weighted_ref is not None:
            weighted_ref[rows, :] = jnp.where(at, weight[e : e + 1, :], 0.0)


def gather_kernel(top, half, capacity, first_ref, info_ref, x_ref, out_ref, pick_ref):
    slot_tables(top, half, capacity, first_ref[0], info_ref[...], pick_ref)
    out_ref[...] = dot(pick_ref[...].astype(BF16), x_ref[...], ((1,), (0,))).astype(BF16)


def cot_kernel(top, half, capacity, first_ref, info_ref, info2_ref, x_ref, x2_ref, out_ref, pick_ref, weight_ref):
    width = x_ref.shape[1]
    lane = lax.broadcasted_iota(jnp.int32, (out_ref.shape[0], LANES), 1)
    facts = jnp.zeros((out_ref.shape[0], LANES), F32)
    for i, (info_in, x) in enumerate(((info_ref, x_ref), (info2_ref, x2_ref))):
        info = info_in[...]
        slot_tables(top, half, capacity, first_ref[0], info, pick_ref, weight_ref)
        pick = pick_ref[...]
        rows = dot(pick.astype(BF16), x[...], ((1,), (0,)))
        out_ref[:, i * width : (i + 1) * width] = rows.astype(BF16)
        share = jnp.sum(weight_ref[...], axis=1, keepdims=True)
        high = share.astype(BF16).astype(F32)
        middle = (share - high).astype(BF16).astype(F32)
        flags = info[2 * top : 2 * top + 2, :]
        marks = [jnp.sum(pick * flags[k : k + 1, :], axis=1, keepdims=True) for k in range(2)]
        counts = jnp.sum(flags, axis=1, keepdims=True)
        columns = [high, middle, share - high - middle, marks[0], marks[1], counts[0:1, :], counts[1:2, :]]
        for k, column in enumerate(columns):
            facts = jnp.where(lane == i * LANES // 2 + k, column, facts)
    out_ref[:, 2 * width :] = facts.astype(BF16)


def spread_kernel(top, half, capacity, first_ref, info_ref, info2_ref, *refs):
    outs, (pick_ref, weight_ref) = refs[:-2], refs[-2:]
    for i, info in enumerate((info_ref, info2_ref)):
        slot_tables(top, half, capacity, first_ref[0], info[...], pick_ref, weight_ref)
        weight = weight_ref[...]
        high = weight.astype(BF16)
        outs[2 * i][...] = high
        outs[2 * i + 1][...] = (weight - high.astype(F32)).astype(BF16)


def mix_kernel(high_ref, low_ref, back_ref, *rest):
    far_refs, out_ref = rest[:-1], rest[-1]
    back = back_ref[...]
    total = dot(high_ref[...], back, ((0,), (0,))) + dot(low_ref[...], back, ((0,), (0,)))
    for far in far_refs:
        total = total + far[...].astype(F32)
    out_ref[...] = total.astype(BF16)


def halve_kernel(core_ref, x_ref, out_ref, sem):
    width = out_ref.shape[1]
    mine = pl.ds(pl.multiple_of(core_ref[0] * width, LANES), width)
    copy = pltpu.make_async_copy(x_ref.at[:, mine], out_ref, sem)
    copy.start()
    copy.wait()


def add_kernel(a_ref, b_ref, out_ref):
    out_ref[...] = (a_ref[...].astype(F32) + b_ref[...].astype(F32)).astype(BF16)


def spans_of(at_ref, first, count, width):
    return [pl.ds(pl.multiple_of(at_ref[first + i], LANES), width) for i in range(count)]


def copier(sems):
    started = []

    def copy(src, dst):
        started.append(pltpu.make_async_copy(src, dst, sems.at[len(started)]))
        started[-1].start()
        return started[-1]

    return copy


def block(ref, j, step):
    return ref.at[pl.ds(j * step, step)]


def stacked(copy, srcs, dst, begin=0):
    slots, width = dst.shape[0] // 2, dst.shape[1]
    if len(srcs) == 1:
        views = [srcs[0].at[:, pl.ds(i * width, width)] for i in range(2)]
    else:
        views = [src.at[:, pl.ds(begin, width)] for src in srcs]
    return [copy(view, block(dst, i, slots)) for i, view in enumerate(views)]


def forward_kernel(pieces, out_pieces, step, at_ref, *refs):
    n = pieces
    xs_in, weights_in, refs = refs[: 2 * n], refs[2 * n : 2 * n + 3], refs[2 * n + 3 :]
    outs, refs = refs[: 3 + 2 * out_pieces], refs[3 + 2 * out_pieces :]
    xs, (gate_w, up_w, down_w), refs = refs[:n], refs[n : n + 3], refs[n + 3 :]
    (keep_gate, keep_up, hidden_ref), own, sems = refs[:3], refs[3:-1], refs[-1]
    copy = copier(sems)
    slots, width = own[0].shape
    spans = spans_of(at_ref, 0, n, xs[0].shape[1])
    out_spans = spans_of(at_ref, n, out_pieces, width)
    blocks = gate_w.shape[0] // step
    x_copies = [started for i, dst in enumerate(xs) for started in stacked(copy, xs_in[i::n], dst)]
    gate_copies, up_copies = [], []
    for j in range(blocks):
        gate_copies.append(copy(block(weights_in[0], j, step), block(gate_w, j, step)))
        up_copies.append(copy(block(weights_in[1], j, step), block(up_w, j, step)))
    down_copy = copy(weights_in[2], down_w)
    for started in x_copies:
        started.wait()
    for j in range(blocks):
        gate_copies[j].wait()
        up_copies[j].wait()
        units = slice(j * step, (j + 1) * step)
        gate = sum(dot(x[...], gate_w[units, span], ((1,), (1,))) for x, span in zip(xs, spans))
        up = sum(dot(x[...], up_w[units, span], ((1,), (1,))) for x, span in zip(xs, spans))
        s = jax.nn.sigmoid(gate)
        silu = gate * s
        keep_gate[:, units] = (up * s * (1.0 + gate * (1.0 - s))).astype(BF16)
        keep_up[:, units] = silu.astype(BF16)
        hidden_ref[:, units] = (silu * up).astype(BF16)
    out_copies = [copy(src, dst) for src, dst in zip((keep_gate, keep_up, hidden_ref), outs[:3])]
    down_copy.wait()
    for i in reversed(range(out_pieces)):
        both = dot(hidden_ref[...], down_w[:, out_spans[i]], ((1,), (0,))).astype(BF16)
        own[i][...] = both[:slots]
        out_copies.append(copy(own[i], outs[3 + out_pieces + i]))
        outs[3 + i][...] = both[slots:]
    for started in out_copies:
        started.wait()


def gradients_kernel(pieces, cot_pieces, capacity, scale, step, at_ref, *refs):
    n, m = pieces, cot_pieces
    cots_in, toks_in, refs = refs[:m], refs[m : m + 2 * n], refs[m + 2 * n :]
    facts_in, inputs, refs = refs[0], refs[1:5], refs[5:]
    outs, cots, toks, refs = refs[:3], refs[3 : 3 + m], refs[3 + m : 3 + m + n], refs[3 + m + n :]
    down_w, keep_gate, keep_up, hidden, dgate, dup, facts_ref, turned, held, sems = refs
    copy = copier(sems)
    spans = spans_of(at_ref, 0, n, toks[0].shape[1])
    spans = spans_of(at_ref, n, m, cots[0].shape[1])
    facts_copy = copy(facts_in.at[:, pl.ds(facts_in.shape[1] - LANES, LANES)], facts_ref)
    hidden_copy = copy(inputs[3], hidden)
    cot_copies = [stacked(copy, [src], dst) for src, dst in zip(cots_in, cots)]
    down_copy = copy(inputs[0], down_w)
    keep_copies = [copy(inputs[1], keep_gate), copy(inputs[2], keep_up)]
    tok_copies = [stacked(copy, toks_in[i::n], dst) for i, dst in enumerate(toks)]
    facts_copy.wait()
    facts = facts_ref[...].astype(F32)
    slots, side = facts.shape[0], LANES // 2
    total = jnp.zeros((1, LANES), F32)
    for row in range(0, slots, capacity):
        total = total + facts[row : row + 1, :]
    retain_all = total[:, 5:6] + total[:, side + 5 : side + 6]
    forget_all = total[:, 6:7] + total[:, side + 6 : side + 7]

    def weight_of(begin):
        share, retain, forget = facts[:, begin : begin + 3], facts[:, begin + 3 : begin + 4], facts[:, begin + 4 : begin + 5]
        coefficient = scale * (retain / retain_all - forget / forget_all)
        return coefficient * (share[:, 0:1] + share[:, 1:2] + share[:, 2:3])

    slot_weights = [weight_of(0), weight_of(side)]
    for i in range(m):
        for started in cot_copies[i]:
            started.wait()
        for part in range(2):
            rows = slice(part * slots, (part + 1) * slots)
            cots[i][rows, :] = (slot_weights[part] * cots[i][rows, :].astype(F32)).astype(BF16)
    done = [[] for _ in range(max(n, m))]
    written = []

    def outer(left, xs, spans, copies, k):
        turned[...] = left[...].T
        for i, (x, span) in enumerate(zip(xs, spans)):
            for started in copies[i]:
                started.wait()
            width = x.shape[1]
            place = slice(i * width, (i + 1) * width)
            held[k, :, place] = dot(turned[...], x[...], ((1,), (0,))).astype(BF16)
            written.append(copy(held.at[k, :, pl.ds(i * width, width)], outs[k].at[:, span]))

    hidden_copy.wait()
    outer(hidden, cots, spans, done, 2)
    down_copy.wait()
    for started in keep_copies:
        started.wait()
    for begin in range(0, down_w.shape[0], step):
        units = slice(begin, begin + step)
        dhidden = sum(dot(x[...], down_w[units, span], ((1,), (1,))) for x, span in zip(cots, spans))
        dgate[:, units] = (dhidden * keep_gate[:, units].astype(F32)).astype(BF16)
        dup[:, units] = (dhidden * keep_up[:, units].astype(F32)).astype(BF16)
    outer(dgate, toks, spans, tok_copies, 0)
    outer(dup, toks, spans, done, 1)
    for started in written:
        started.wait()


def body(
    tokens,
    cotangent,
    expert_ids,
    route_weight,
    forget_mask,
    lengths,
    gate_weight,
    up_weight,
    down_weight,
):
    tok_rows, features = tokens.shape
    top = expert_ids.shape[1]
    owners = lax.axis_size("dp")
    parts = lax.axis_size("tensor")
    half = owners // 2
    width = features // parts
    capacity = 5 * tok_rows * top // (4 * owners)
    slots = half * capacity
    seq_len = tok_rows * owners // lengths.shape[0]
    me = lax.axis_index("dp")
    core = lax.axis_index("tensor")
    mates = [(i, (i + half) % owners) for i in range(owners)]
    halves = [list(range(half)), list(range(half, owners))]
    first = ((me // half) * half).astype(jnp.int32).reshape(1)
    place = (me * tok_rows).astype(jnp.int32).reshape(1)
    shape = jax.ShapeDtypeStruct
    table = pltpu.VMEM((slots, tok_rows), F32)
    limit = pltpu.CompilerParams(vmem_limit_bytes=8 * 2**20)

    def to_mate(value):
        return lax.ppermute(value, "dp", mates)

    def exchange(value):
        value = value.reshape(half, value.shape[0] // half, value.shape[1])
        return lax.all_to_all(
            value, "dp", split_axis=0, concat_axis=0, axis_index_groups=halves, tiled=True
        )

    def swapped(value):
        return lax.ppermute(value, "tensor", [(0, 1), (1, 0)])

    def my_features(value, micros):
        return pl.pallas_call(
            halve_kernel,
            out_shape=shape((tok_rows, width), BF16),
            in_specs=[SMEM, HBM],
            out_specs=VMEM,
            scratch_shapes=[pltpu.SemaphoreType.DMA],
            compiler_params=limit,
            cost_estimate=cost(micros),
        )(core.astype(jnp.int32).reshape(1), in_hbm(value))

    def after(value, *others):
        return lax.optimization_barrier((value, *others))[0]

    def mixed_rows(spread, back, *far):
        return pl.pallas_call(
            mix_kernel,
            out_shape=shape((tok_rows, width), BF16),
            in_specs=[VMEM] * (3 + len(far)),
            out_specs=VMEM,
            compiler_params=limit,
            cost_estimate=cost(1),
        )(*spread, back, *far)

    tok_mine = my_features(tokens, 1)
    tok_mate = to_mate(tok_mine)
    expert_ids = after(expert_ids, tok_mine)
    about = pl.pallas_call(
        functools.partial(facts_kernel, top, seq_len),
        out_shape=jax.ShapeDtypeStruct((FACTS, tok_rows), F32),
        in_specs=[SMEM, SMEM, VMEM, VMEM, VMEM],
        out_specs=VMEM,
        compiler_params=limit,
        cost_estimate=cost(1),
    )(place, lengths, expert_ids.T, route_weight.T, forget_mask.reshape(1, tok_rows))
    about_mate = to_mate(about)

    def gathered(info, x, micros):
        return pl.pallas_call(
            functools.partial(gather_kernel, top, half, capacity),
            out_shape=shape((slots, width), BF16),
            in_specs=[SMEM, VMEM, VMEM],
            out_specs=VMEM,
            scratch_shapes=[table],
            compiler_params=limit,
            cost_estimate=cost(micros),
        )(first, info, x)

    recv_own = exchange(gathered(about, tok_mine, 1)).reshape(slots, width)
    send_mate = gathered(about_mate, tok_mate, 20)
    recv_mate = exchange(after(send_mate, recv_own)).reshape(slots, width)

    spreads = pl.pallas_call(
        functools.partial(spread_kernel, top, half, capacity),
        out_shape=[shape((slots, tok_rows), BF16)] * 4,
        in_specs=[SMEM, VMEM, VMEM],
        out_specs=[VMEM] * 4,
        scratch_shapes=[table, table],
        compiler_params=limit,
        cost_estimate=cost(1),
    )(first, about, about_mate)

    cot_mine = my_features(after(cotangent, about), 1)
    cot_mate = to_mate(after(cot_mine, send_mate))
    send_cot = pl.pallas_call(
        functools.partial(cot_kernel, top, half, capacity),
        out_shape=shape((slots, 2 * width + LANES), BF16),
        in_specs=[SMEM] + [VMEM] * 4,
        out_specs=VMEM,
        scratch_shapes=[table, table],
        compiler_params=limit,
        cost_estimate=cost(15),
    )(first, about, about_mate, cot_mine, cot_mate)
    recv_own, recv_mate = after(recv_own, send_cot), after(recv_mate, send_cot)
    recv_cot = exchange(after(send_cot, recv_mate)).reshape(slots, 2 * width + LANES)

    gate_w, up_w, down_w = gate_weight[0], up_weight[0], down_weight[0]
    weights = [in_hbm(w) for w in (gate_w, up_w, down_w)]
    units = gate_w.shape[0]
    step = min(units, 256)
    blocks = units // step

    def all_features(row):
        return lax.all_gather(row, "tensor", axis=1, tiled=True)

    if parts == 2:
        other_own = swapped(recv_own)
        toks = [recv_own, other_own, recv_mate, swapped(after(recv_mate, other_own))]
        starts = [core * width, (1 - core) * width] * 2
        span = width
    else:
        toks = [all_features(recv_own), all_features(recv_mate)]
        starts = [core * 0] * 2
        span = features
    at = jnp.stack(starts).astype(jnp.int32)
    toks = [in_hbm(x) for x in toks]
    n = m = len(toks) // 2
    weight_buffer = pltpu.VMEM((units, features), BF16)
    unit_rows = ((2 * slots, units), BF16)
    tok_buffers = [pltpu.VMEM((2 * slots, span), BF16)] * n
    cot_buffers = [pltpu.VMEM((2 * slots, span), BF16)] * m
    roomy = pltpu.CompilerParams(vmem_limit_bytes=36 * 2**20)

    def summed(outs):
        if parts != 2:
            return lax.psum_scatter(outs[0], "tensor", scatter_dimension=1, tiled=True)
        return pl.pallas_call(
            add_kernel,
            out_shape=shape((slots, width), BF16),
            in_specs=[VMEM] * 2,
            out_specs=VMEM,
            compiler_params=limit,
            cost_estimate=cost(1),
        )(outs[0], swapped(outs[1]))

    piece = (slots, span)
    keep_gate, keep_up, hidden, *outs = pl.pallas_call(
        functools.partial(forward_kernel, n, m, step),
        out_shape=[pltpu.HBM(*unit_rows)] * 3
        + [shape(piece, BF16)] * m
        + [pltpu.HBM(piece, BF16)] * m,
        in_specs=[SMEM] + [HBM] * (2 * n + 3),
        out_specs=[HBM] * 3 + [VMEM] * m + [HBM] * m,
        scratch_shapes=tok_buffers
        + [weight_buffer] * 3
        + [pltpu.VMEM(*unit_rows)] * 3
        + [pltpu.VMEM(piece, BF16)] * m
        + [pltpu.SemaphoreType.DMA((2 * n + 2 * blocks + 4 + m,))],
        compiler_params=roomy,
        cost_estimate=cost(8),
    )(at, *toks, *weights)
    out_mate = summed(outs[:m])
    back_mate = exchange(out_mate).reshape(slots, width)
    out_own = summed(outs[m:])

    recv_cot = after(recv_cot, out_mate)
    if parts == 2:
        cots = [recv_cot, swapped(recv_cot)]
    else:
        both = [all_features(recv_cot[:, i * width : (i + 1) * width]) for i in range(2)]
        cots = [jnp.concatenate(both, axis=1)]
    mix_mate = mixed_rows(spreads[2:], back_mate)
    mix_far = to_mate(mix_mate)
    keeps = [in_hbm(x) for x in (keep_gate, keep_up, after(hidden, mix_mate))]
    grad_gate, grad_up, grad_down = pl.pallas_call(
        functools.partial(gradients_kernel, n, m, capacity, float(top * tok_rows), step),
        out_shape=[pltpu.HBM((units, features), BF16)] * 3,
        in_specs=[SMEM] + [HBM] * (2 * n + m + 5),
        out_specs=[HBM] * 3,
        scratch_shapes=cot_buffers
        + tok_buffers
        + [weight_buffer]
        + [pltpu.VMEM(*unit_rows)] * 5
        + [
            pltpu.VMEM((slots, LANES), BF16),
            pltpu.VMEM((units, 2 * slots), BF16),
            pltpu.VMEM((3, units, features), BF16),
            pltpu.SemaphoreType.DMA((4 * n + 3 * m + 5,)),
        ],
        compiler_params=roomy,
        cost_estimate=cost(12),
    )(at, *[in_hbm(x) for x in cots], *toks, in_hbm(recv_cot), weights[2], *keeps)
    back_own = exchange(after(out_own, back_mate)).reshape(slots, width)
    mixed = mixed_rows([after(spreads[0], grad_down), spreads[1]], back_own, mix_far)
    return (
        mixed,
        grad_gate[None],
        grad_up[None],
        grad_down[None],
    )


def solution(mesh):
    in_specs = (
        P("dp", None),
        P("dp", None),
        P("dp", None),
        P("dp", None),
        P("dp"),
        P(),
        P("dp", "tensor", None),
        P("dp", "tensor", None),
        P("dp", "tensor", None),
    )
    out_specs = (
        P("dp", "tensor"),
        P("dp", "tensor", None),
        P("dp", "tensor", None),
        P("dp", "tensor", None),
    )
    return jax.shard_map(body, mesh=mesh, in_specs=in_specs, out_specs=out_specs, check_vma=False)
```
